256 devices in a mesh: gx: 16 (over y, x), gy: 16 (over z, core).
Axes of the slice: x: 4, y: 4, z: 8, core: 2. Of those that a mesh axis runs over, the one named last changes fastest.
Arguments:
- innovation: float32 [68, 256, 4096], P(None, 'gx', 'gy'), may hold values from -6 to 6
- area: float32 [256, 4096], P('gx', 'gy'), may hold values from 0.5 to 2
- spread_sd: float32 [68, 64, 2048], P(None, 'gx', 'gy'), may hold values from 0.3 to 3
- smooth_coef: float32 [68], replicated, may hold values from 0.04 to 0.22
- obs_column: int32 [262144], P(('gx', 'gy')), may hold values from 0 to 511
- obs_weight: float32 [68, 262144], P(None, ('gx', 'gy')), may hold values from -0.75 to 0.75
- obs_precision: float32 [262144], P(('gx', 'gy')), may hold values from 0.5 to 4
- obs_live: int32 [262144], P(('gx', 'gy')), may hold values from 0 to 1, as said below
Outputs:
- fine_increment: float32 [68, 256, 4096], P(None, 'gx', 'gy')
- control: float32 [68, 64, 2048], P(None, 'gx', 'gy')
The draws below stay inside these ranges and needn't reach their ends.
Inputs may be any that keep to these rules, and one draw needn't show every extreme that they name: obs_column is the index, inside the coarse tile of the tile that holds the slot, of the observed column, longitude-major (128 per row). `obs_live`: within each tile's block of 1024 slots the live ones come first; every block holds 128 or more, and some block is full.
All inputs are finite; a program needn't handle non-finite values.
Results may differ from the reference program's by a relative error of at most 0.0001.
Values sent between devices are 32-bit elements; how exact they have to be, the bound alone decides.
A program may use at most 64 MiB of HBM per device.

```python
import math
import jax
import jax.numpy as jnp

PLANES = 68
RX = 4
RY = 2
OBS_DEV = 1024
ITERS = 3
CX = 4
CY = 128
NXF = 256
NYF = 4096
NXC = 64
NYC = 2048
NOBS = 262144
N_GY = 16


def draw_obs_live(key, part):
    key = jax.random.fold_in(key, 11)
    count_key, full_key = jax.random.split(key)
    blocks = NOBS // OBS_DEV
    counts = jax.random.randint(count_key, (blocks,), OBS_DEV // 8, OBS_DEV + 1)
    full_block = jax.random.randint(full_key, (), 0, blocks)
    counts = jnp.where(jnp.arange(blocks) == full_block, OBS_DEV, counts)
    slots = jnp.arange(NOBS) % OBS_DEV
    return (slots < jnp.repeat(counts, OBS_DEV)).astype(jnp.int32)


def plant(array, stream_key, low, largest):
    longest = array.shape.index(max(array.shape))
    spots = []
    for shift in (0, 1):
        where = [jax.random.randint(jax.random.fold_in(stream_key, axis), (), 0, length) for axis, length in enumerate(array.shape)]
        where[longest] = (where[longest] + shift) % array.shape[longest]
        spots.append(tuple(where))
    return array.at[spots[0]].set(low).at[spots[1]].set(largest)


def levels(stream_key, extent, cuts, low, top_value):
    level, own = 1.0, jax.random.fold_in(stream_key, 6)
    for dim, blocks in cuts:
        heights = jnp.exp(jax.random.uniform(jax.random.fold_in(own, dim), (blocks,), jnp.float32, low / len(cuts), top_value / len(cuts)))
        level = level * jnp.repeat(heights, extent[dim] // blocks).reshape([-1 if axis == dim else 1 for axis in range(len(extent))])
    return level


def centred(key, extent, deviation, most, shards=(), kind=jnp.bfloat16):
    values = deviation * jax.random.normal(key, extent, jnp.float32)
    if shards:
        values = values * levels(key, extent, shards, -0.22, 0.18)
    return jnp.clip(values, -most, most).astype(kind)


def setup_inputs(seed: int = 0) -> dict:
    arg_keys = jax.random.split(jax.random.key(seed), 9)
    return {
        "innovation": centred(arg_keys[0], (PLANES, NXF, NYF), 1.0, 6.0, ((1, 16), (2, 16)), jnp.float32),
        "area": jnp.clip(jnp.exp(math.log(2.0) - 1.3862944 * jax.random.uniform(arg_keys[1], (NXF, NYF), jnp.float32) ** levels(arg_keys[1], (NXF, NYF), ((0, 16), (1, 16)), -0.2, 0.2)), 0.5, 2.0),
        "spread_sd": jnp.clip(jnp.exp(math.log(3.0) - 2.3025851 * jax.random.uniform(arg_keys[2], (PLANES, NXC, NYC), jnp.float32) ** levels(arg_keys[2], (PLANES, NXC, NYC), ((1, 16), (2, 16)), -0.2, 0.2)), 0.3, 3.0),
        "smooth_coef": jnp.clip(jnp.exp(jax.random.uniform(arg_keys[3], (PLANES,), jnp.float32, math.log(0.04), math.log(0.22))), 0.04, 0.22),
        "obs_column": plant(jax.random.randint(arg_keys[4], (NOBS,), 0, CX * CY), jax.random.fold_in(arg_keys[4], 1), 0, (CX * CY) - 1).astype(jnp.int32),
        "obs_weight": centred(arg_keys[5], (PLANES, NOBS), PLANES ** -0.5, 0.75, ((1, 256),), jnp.float32),
        "obs_precision": jnp.clip(jnp.exp(math.log(4.0) - 2.0794415 * jax.random.uniform(arg_keys[6], (NOBS,), jnp.float32) ** levels(arg_keys[6], (NOBS,), ((0, 256),), -0.2, 0.2)), 0.5, 4.0),
        "obs_live": draw_obs_live(jax.random.fold_in(arg_keys[8], 71), 0),
    }


def tap_weights(ratio):
    return [0.5 / (ratio + 1.0)] + [1.0 / (ratio + 1.0)] * ratio + [0.5 / (ratio + 1.0)]


def restrict(padded, coarse_x, coarse_y):
    weights_x = tap_weights(RX)
    weights_y = tap_weights(RY)
    along_x = weights_x[0] * padded[:, 0:RX * (coarse_x - 1) + 1:RX, :]
    for offset in range(1, RX + 2):
        along_x = along_x + weights_x[offset] * padded[:, offset:offset + RX * (coarse_x - 1) + 1:RX, :]
    result = weights_y[0] * along_x[:, :, 0:RY * (coarse_y - 1) + 1:RY]
    for offset in range(1, RY + 2):
        result = result + weights_y[offset] * along_x[:, :, offset:offset + RY * (coarse_y - 1) + 1:RY]
    return result


def spread(coarse):
    planes, coarse_x, coarse_y = coarse.shape
    weights_x = tap_weights(RX)
    weights_y = tap_weights(RY)
    middle = jnp.zeros((planes, coarse_x, RY * coarse_y + 2), jnp.float32)
    for offset in range(RY + 2):
        middle = middle.at[:, :, offset:offset + RY * (coarse_y - 1) + 1:RY].add(weights_y[offset] * coarse)
    result = jnp.zeros((planes, RX * coarse_x + 2, RY * coarse_y + 2), jnp.float32)
    for offset in range(RX + 2):
        result = result.at[:, offset:offset + RX * (coarse_x - 1) + 1:RX, :].add(weights_x[offset] * middle)
    return result


def smooth_padded(padded, smooth_coef):
    middle = padded[:, 1:-1, 1:-1]
    beside = padded[:, 2:, 1:-1] + padded[:, :-2, 1:-1] + padded[:, 1:-1, 2:] + padded[:, 1:-1, :-2]
    return (1.0 - 4.0 * smooth_coef)[:, None, None] * middle + smooth_coef[:, None, None] * beside


def smooth_twice(field, smooth_coef):
    for repeat in range(2):
        field = smooth_padded(jnp.pad(field, ((0, 0), (1, 1), (1, 1))), smooth_coef)
    return field


def observe(field, cells, obs_weight, obs_scale):
    columns = field.reshape(field.shape[0], -1)
    picked = jnp.take(columns, cells, axis=1)
    values = jnp.sum(obs_weight * picked, axis=0) * obs_scale
    return jnp.zeros_like(columns).at[:, cells].add(obs_weight * values[None, :]).reshape(field.shape)


def global_columns(obs_column):
    slots = jnp.arange(NOBS, dtype=jnp.int32)
    block = slots // OBS_DEV
    row_index = (block // N_GY) * CX + obs_column // CY
    col_index = (block % N_GY) * CY + obs_column % CY
    return (row_index * NYC + col_index).astype(jnp.int32)


def reference(innovation, area, spread_sd, smooth_coef, obs_column, obs_weight, obs_precision, obs_live):
    cells = global_columns(obs_column)
    obs_scale = obs_precision * obs_live.astype(jnp.float32)

    def hessian(vector):
        pushed = spread_sd * smooth_twice(vector, smooth_coef)
        return vector + smooth_twice(spread_sd * observe(pushed, cells, obs_weight, obs_scale), smooth_coef)

    padded = jnp.pad(innovation * area[None, :, :], ((0, 0), (1, 1), (1, 1)))
    forcing = restrict(padded, NXC, NYC)
    right_side = smooth_twice(spread_sd * forcing, smooth_coef)
    control = jnp.zeros_like(right_side)
    resid = right_side
    direction = right_side
    norm_now = jnp.sum(resid * resid)
    for section in range(ITERS):
        hess_dir = hessian(direction)
        step_len = norm_now / jnp.sum(direction * hess_dir)
        control = control + step_len * direction
        resid = resid - step_len * hess_dir
        norm_next = jnp.sum(resid * resid)
        direction = resid + (norm_next / norm_now) * direction
        norm_now = norm_next
    increment = spread_sd * smooth_twice(control, smooth_coef)
    fine_increment = spread(increment)[:, 1:-1, 1:-1]
    return fine_increment, control
```

```python
import functools

import jax
import jax.numpy as jnp
from jax import lax
from jax.experimental import pallas as pl
from jax.experimental.pallas import tpu as pltpu
from jax.sharding import PartitionSpec as P

F32 = jnp.float32
BF16 = jnp.bfloat16
MESH = pl.DeviceIdType.MESH
PLANES = 68
PAD = 72
MPAD = 80
GROUPS = PAD // 8
SIDES = [(sx, sy) for sx in (-1, 0, 1) for sy in (-1, 1)]


def pieces(x):
    high = x.astype(BF16)
    rest = x - high.astype(F32)
    middle = rest.astype(BF16)
    low = (rest - middle.astype(F32)).astype(BF16)
    return jnp.concatenate([high, middle, low], axis=0)


def dot(a, b):
    return jnp.dot(a, b, preferred_element_type=F32)


def iota(shape, dim):
    return lax.broadcasted_iota(jnp.int32, shape, dim)


def tap(offset, ratio):
    inner = (offset >= 0) & (offset < ratio)
    ends = (offset == -1) | (offset == ratio)
    return jnp.where(inner, 2.0, jnp.where(ends, 1.0, 0.0))


def coarse_lane(lane):
    return jnp.where(lane == 255, -1, lane)


def roll(x, shift):
    return pltpu.roll(x, shift % 128, x.ndim - 1)


def beside(low, high, lane):
    low_up, low_down = roll(low, 1), roll(low, 127)
    high_up, high_down = roll(high, 1), roll(high, 127)
    first, last = lane == 0, lane == 127
    of_low = jnp.where(first, high_up, low_up) + jnp.where(last, high_down, low_down)
    of_high = jnp.where(first, low_up, high_up) + jnp.where(last, low_down, high_down)
    return of_low, of_high


def solve(
    nx,
    ny,
    inn_hbm,
    area_hbm,
    sd_hbm,
    coef_ref,
    col_ref,
    weight_hbm,
    prec_ref,
    live_ref,
    inc_low,
    inc_high,
    ctl,
    inn,
    area,
    sd_in,
    sd,
    weight,
    coef_a,
    coef_b,
    pick,
    place,
    taps_y,
    along,
    rest_low,
    rest_high,
    rim_in,
    field,
    packed,
    packed_in,
    res_low,
    res_high,
    dir_low,
    dir_high,
    ured,
    gathered,
    scaled,
    msg_a,
    msg_b,
    slots_a,
    slots_b,
    in_sems,
    x_send,
    x_recv,
    p_send,
    p_recv,
    a_send,
    a_recv,
    b_send,
    b_recv,
):
    gx, gy = lax.axis_index("gx"), lax.axis_index("gy")

    def at(dx, dy):
        return (lax.rem(gx + dx + nx, nx), lax.rem(gy + dy + ny, ny))

    loads = [
        pltpu.make_async_copy(inn_hbm, inn.at[pl.ds(0, PLANES)], in_sems.at[0]),
        pltpu.make_async_copy(area_hbm, area, in_sems.at[1]),
        pltpu.make_async_copy(sd_hbm, sd_in, in_sems.at[2]),
        pltpu.make_async_copy(weight_hbm, weight, in_sems.at[3]),
    ]
    for load in loads:
        load.start()

    barrier = pltpu.get_barrier_semaphore()
    partners = [at(0, o) for o in range(1, ny)] + [at(o, 0) for o in range(1, nx)]
    partners += [at(dx, dy) for dx in (-1, 1) for dy in (-1, 1)]
    for partner in partners:
        pl.semaphore_signal(barrier, inc=1, device_id=partner, device_id_type=MESH)

    lane8 = iota((8, 128), 1)
    left_ok, right_ok = gx > 0, gx < nx - 1
    low_ok, high_ok = gy > 0, gy < ny - 1
    edge_f = jnp.where(lane8 < 64, jnp.where(high_ok, 1.0, 0.0), jnp.where(low_ok, 1.0, 0.0))
    left_f, right_f = jnp.where(left_ok, 1.0, 0.0), jnp.where(right_ok, 1.0, 0.0)

    inn[PLANES:] = jnp.zeros((PAD - PLANES, 16, 256), F32)
    gathered[PAD:] = jnp.zeros((MPAD - PAD, 512), F32)
    diagonal = iota((PAD, PLANES), 0) == iota((PAD, PLANES), 1)
    coef = jnp.sum(
        jnp.where(diagonal, jnp.broadcast_to(coef_ref[...], (PAD, PLANES)), 0.0),
        axis=1,
        keepdims=True,
    )
    coef_b[...] = jnp.broadcast_to(coef, (PAD, 128))
    coef_a[...] = jnp.broadcast_to(1.0 - 4.0 * coef, (PAD, 128))

    out_row, in_row = iota((48, 384), 0), iota((48, 384), 1) & 127
    same = (out_row & 7) == (in_row >> 4)
    off = (in_row & 15) - 4 * ((out_row >> 3) - 1)
    taps_x = jnp.where(same, tap(off, 4), 0.0).astype(BF16)
    taps_y[...] = tap(iota((256, 256), 0) - 2 * coarse_lane(iota((256, 256), 1)), 2).astype(BF16)

    loads[0].wait()
    loads[1].wait()

    def restrict_x(g, carry):
        at_g = pl.ds(pl.multiple_of(g * 8, 8), 8)
        block = (inn[at_g] * area[...][None]).reshape(128, 256)
        along[:, at_g, :] = dot(taps_x, pieces(block)).reshape(6, 8, 256)
        return carry

    lax.fori_loop(0, GROUPS, restrict_x, 0, unroll=3)
    part = dot(pieces(along[...].reshape(6 * PAD, 256)), taps_y[...])
    part = (part[: 6 * PAD] + part[6 * PAD : 12 * PAD] + part[12 * PAD :]) * (1.0 / 60.0)
    rest_low[...] = part[:, :128].reshape(6, PAD, 128)
    rest_high[...] = part[:, 128:].reshape(6, PAD, 128)

    edge = jnp.zeros((PAD, 128), F32)
    for r in range(6):
        edge = edge + roll(rest_high[r], 1 + 2 * r)
    packed[0] = edge

    pl.semaphore_wait(barrier, len(partners))

    def remote(source, target, send, recv, device):
        copy = pltpu.make_async_remote_copy(
            src_ref=source,
            dst_ref=target,
            send_sem=send,
            recv_sem=recv,
            device_id=device,
            device_id_type=MESH,
        )
        copy.start()
        return copy

    sent = []

    def exchange(e, to_left, at_right, to_right, at_left):
        copies = [
            remote(to_left, at_right, x_send.at[e, 0], x_recv.at[e, 1], at(-1, 0)),
            remote(to_right, at_left, x_send.at[e, 1], x_recv.at[e, 0], at(1, 0)),
        ]
        for n, (sx, sy) in enumerate(SIDES):
            copies.append(
                remote(
                    packed.at[e], packed_in.at[e, n], p_send.at[e, n], p_recv.at[e, n], at(-sx, -sy)
                )
            )
        sent.extend(copies)
        return copies

    def arrived(copies):
        for copy in copies:
            copy.wait_recv()

    def sides(e, at_g, above):
        result = []
        for sx, ok in ((-1, left_ok), (0, None), (1, right_ok)):
            n = 2 * (sx + 1)
            both = jnp.where(above, packed_in[e, n + 1, at_g, :], packed_in[e, n, at_g, :])
            inside = jnp.where(above, jnp.where(high_ok, 1.0, 0.0), jnp.where(low_ok, 1.0, 0.0))
            if ok is not None:
                inside = inside * jnp.where(ok, 1.0, 0.0)
            result.append(jnp.where(inside > 0.5, both, 0.0))
        return result

    copies = exchange(0, rest_low.at[0], rim_in.at[1], rest_low.at[5], rim_in.at[0])

    loads[2].wait()
    loads[3].wait()
    for i in range(4):
        sd[i, :PLANES] = sd_in[:, i, :]
        sd[i, PLANES:] = jnp.zeros((PAD - PLANES, 128), F32)
    cols = col_ref[...]
    cols_t = jnp.transpose(jnp.concatenate([cols.astype(F32), jnp.zeros((120, 128), F32)], axis=0))
    column = iota((512, 128), 0)
    for a in range(8):
        k = pl.ds(128 * a, 128)
        pick[:, k] = jnp.where(column == cols[a : a + 1], 1.0, 0.0).astype(BF16)
        of_slot = jnp.broadcast_to(cols_t[:, a : a + 1], (128, 512))
        place[k, :] = jnp.where(of_slot == iota((128, 512), 1).astype(F32), 1.0, 0.0).astype(BF16)
    obs_scale = prec_ref[...] * live_ref[...].astype(F32)

    arrived(copies)

    def force(g, carry):
        at_g = pl.ds(pl.multiple_of(g * 8, 8), 8)
        rim = sides(0, at_g, (lane8 & 1) == 0)
        ends = (lane8 == 0) | (lane8 == 127)
        for i in range(4):
            value = rest_low[i + 1, at_g, :]
            tails = roll(rim[1], -(2 * (i + 1) + 1))
            if i == 0:
                value = value + rim_in[0, at_g, :] * left_f
                tails = tails + roll(rim[0], -11)
            if i == 3:
                value = value + rim_in[1, at_g, :] * right_f
                tails = tails + roll(rim[2], -1)
            value = value + jnp.where(ends, tails, 0.0)
            field[0, 4 + i, at_g, :] = sd[i, at_g, :] * value
        return carry

    lax.fori_loop(0, GROUPS, force, 0, unroll=3)

    def pack_and_send(e):
        def pack(g, carry):
            at_g = pl.ds(pl.multiple_of(g * 8, 8), 8)
            value = jnp.zeros((8, 128), F32)
            for i in range(4):
                value = jnp.where(
                    (lane8 >> 3) == i, roll(field[e, 4 + i, at_g, :], 4 + 8 * i), value
                )
            packed[1 + e, at_g, :] = value
            return carry

        lax.fori_loop(0, GROUPS, pack, 0, unroll=9)
        own = field.at[e, pl.ds(4, 4)]
        return exchange(1 + e, own, field.at[e, pl.ds(8, 4)], own, field.at[e, pl.ds(0, 4)])

    def smooth(rows, first, coefs):
        result = []
        for n in range(1, len(rows) - 1):
            i = first + n
            a, b, a_high, b_high = coefs[0 if i < 0 else 1 if i < 4 else 2]
            (low, high), before, after = rows[n], rows[n - 1], rows[n + 1]
            of_low, of_high = beside(low, high, lane8)
            of_low = of_low + before[0] + after[0]
            of_high = of_high + before[1] + after[1]
            result.append((a * low + b * of_low, a_high * high + b_high * of_high))
        return result

    def smooth_step(e, alpha, beta):
        def step(g, norm):
            at_g = pl.ds(pl.multiple_of(g * 8, 8), 8)
            odd = (lane8 & 4) == 4
            tails = sides(1 + e, at_g, odd)
            rows = []
            for r in range(12):
                low = field[e, r, at_g, :]
                if r < 4:
                    low = jnp.where(left_f > 0.5, low, 0.0)
                if r >= 8:
                    low = jnp.where(right_f > 0.5, low, 0.0)
                rows.append((low, roll(tails[r // 4], -(8 * (r % 4) + 4))))
            a, b = coef_a[at_g, :], coef_b[at_g, :]
            coefs = [
                (a * f, b * f, a * f * edge_f, b * f * edge_f) for f in (left_f, F32(1.0), right_f)
            ]
            rows = smooth(smooth(rows, -4, coefs), -3, coefs)
            values = []
            for q, (low, high) in enumerate(rows):
                if e > 0:
                    old_low, old_high = res_low[e - 1, q, at_g, :], res_high[e - 1, q, at_g, :]
                    low, high = low + old_low, high + old_high
                    if e > 1:
                        low = low + beta * dir_low[q, at_g, :]
                        high = high + beta * dir_high[q, at_g, :]
                    else:
                        dir_low[q, at_g, :] = low
                        dir_high[q, at_g, :] = high
                    low, high = old_low - alpha * low, old_high - alpha * high
                res_low[e, q, at_g, :] = low
                res_high[e, q, at_g, :] = high
                values.append((low, high))
                if 2 <= q < 6:
                    norm = norm + low * low
            values = smooth(smooth(values, -2, coefs), -1, coefs)
            for i, (low, _) in enumerate(values):
                pushed = sd[i, at_g, :] * low
                ured[1 + i, e, at_g, :] = pushed
                gathered[at_g, pl.ds(128 * i, 128)] = pushed
            return norm

        return lax.fori_loop(0, GROUPS, step, jnp.zeros((8, 128), F32), unroll=1)

    def observe(e, norm):
        left = pieces(gathered[...])
        total = jnp.zeros((1, 128), F32)
        live = iota((PLANES, 256), 0) >= 0
        for n in range(4):
            k = pl.ds(256 * n, 256)
            taken = dot(left, pick[:, k])
            taken = taken[:MPAD] + taken[MPAD : 2 * MPAD] + taken[2 * MPAD :]
            w = weight[:, k]
            seen = jnp.sum(w * taken[:PLANES], axis=0, keepdims=True)
            scale = jnp.concatenate(
                [obs_scale[2 * n : 2 * n + 1], obs_scale[2 * n + 1 : 2 * n + 2]], axis=1
            )
            value = scale * seen
            square = value * seen
            total = total + square[:, :128] + square[:, 128:]
            if e < 2:
                back = jnp.concatenate([w * value, jnp.zeros((MPAD - PLANES, 256), F32)], axis=0)
                scaled[:, k] = pieces(back)
        msg_a[e] = jnp.concatenate([jnp.sum(norm, axis=0, keepdims=True), total], axis=0)

    def put_back(e):
        for h in range(2):
            value = dot(scaled[...], place[:, 256 * h : 256 * h + 256])
            value = value[:PAD] + value[MPAD : MPAD + PAD] + value[2 * MPAD : 2 * MPAD + PAD]
            for i in (2 * h, 2 * h + 1):
                field[e, 4 + i] = sd[i] * value[:, 128 * (i % 2) : 128 * (i % 2) + 128]

    def reduce_start(k, msg, slots, send, recv, count, mine, partner):
        slots[k, mine] = msg[k]
        for o in range(1, count):
            remote(msg.at[k], slots.at[k, mine], send.at[k], recv.at[k], partner(o))

    def reduce_end(k, slots, send, recv, count, partner):
        several = slots.at[k, pl.ds(0, count - 1)]
        whole = pltpu.make_async_remote_copy(
            src_ref=several,
            dst_ref=several,
            send_sem=send.at[k],
            recv_sem=recv.at[k],
            device_id=partner(1),
            device_id_type=MESH,
        )
        whole.wait_recv()
        whole.wait_send()
        total = slots[k, 0]
        for o in range(1, count):
            total = total + slots[k, o]
        return total

    def start_a(k):
        reduce_start(k, msg_a, slots_a, a_send, a_recv, ny, gy, lambda o: at(0, o))

    def turn(k):
        msg_b[k] = reduce_end(k, slots_a, a_send, a_recv, ny, lambda o: at(0, o))
        reduce_start(k, msg_b, slots_b, b_send, b_recv, nx, gx, lambda o: at(o, 0))

    def end_b(k):
        total = reduce_end(k, slots_b, b_send, b_recv, nx, lambda o: at(o, 0))
        total = jnp.sum(total, axis=1, keepdims=True)
        gamma = jnp.broadcast_to(total[0:1], (8, 128))
        return gamma, gamma + jnp.broadcast_to(total[1:2], (8, 128))

    copies = pack_and_send(0)
    arrived(copies)
    norm = smooth_step(0, None, None)
    observe(0, norm)
    start_a(0)
    put_back(1)
    copies = pack_and_send(1)
    turn(0)
    arrived(copies)
    gamma0, delta0 = end_b(0)
    alpha0 = gamma0 / delta0

    norm = smooth_step(1, alpha0, None)
    observe(1, norm)
    start_a(1)
    put_back(2)
    copies = pack_and_send(2)
    turn(1)
    arrived(copies)
    gamma1, delta1 = end_b(1)
    beta1 = gamma1 / gamma0
    alpha1 = gamma1 / (delta1 - beta1 * gamma1 / alpha0)

    norm = smooth_step(2, alpha1, beta1)
    observe(2, norm)
    start_a(2)

    def pack_rims(g, carry):
        at_g = pl.ds(pl.multiple_of(g * 8, 8), 8)
        value = jnp.zeros((8, 128), F32)
        for v in range(3):
            for i in range(4):
                n = 4 * v + i
                value = jnp.where((lane8 >> 1) == n, roll(ured[1 + i, v, at_g, :], 1 + 2 * n), value)
        packed[4, at_g, :] = value
        return carry

    lax.fori_loop(0, GROUPS, pack_rims, 0, unroll=3)
    copies = exchange(4, ured.at[1], ured.at[5], ured.at[4], ured.at[0])
    turn(2)
    arrived(copies)
    gamma2, delta2 = end_b(2)
    beta2 = gamma2 / gamma1
    alpha2 = gamma2 / (delta2 - beta2 * gamma2 / alpha1)
    parts = [alpha0 + beta1 * (alpha1 + alpha2 * beta2), alpha1 + alpha2 * beta2, alpha2]

    def combine(g, carry):
        at_g = pl.ds(pl.multiple_of(g * 8, 8), 8)
        for i in range(4):
            ctl[i, at_g, :] = (
                parts[0] * res_low[0, 2 + i, at_g, :]
                + parts[1] * res_low[1, 2 + i, at_g, :]
                + parts[2] * res_low[2, 2 + i, at_g, :]
            )
        for r in range(6):
            value = (
                parts[0] * ured[r, 0, at_g, :]
                + parts[1] * ured[r, 1, at_g, :]
                + parts[2] * ured[r, 2, at_g, :]
            )
            if r == 0:
                value = jnp.where(left_f > 0.5, value, 0.0)
            if r == 5:
                value = jnp.where(right_f > 0.5, value, 0.0)
            inc_low[r, at_g, :] = value
        odd = (lane8 & 1) == 1
        of_lane = jnp.where(lane8 < 8, parts[0], jnp.where(lane8 < 16, parts[1], parts[2]))
        tails = []
        for value in sides(4, at_g, odd):
            value = value * of_lane
            tails.append(value + roll(value, -8) + roll(value, -16))
        for r in range(6):
            i = (r - 1) % 4
            sx = 0 if r == 0 else 2 if r == 5 else 1
            inc_high[r, at_g, :] = roll(tails[sx], -(2 * i + 1))
        return carry

    lax.fori_loop(0, GROUPS, combine, 0, unroll=1)
    for copy in sent:
        copy.wait_send()


def finish(inc_low, inc_high, ctl, fine_hbm, control, along, fine, sems):
    lane, row = iota((256, 256), 0), iota((256, 256), 1)
    taps_y = tap(row - 2 * coarse_lane(lane), 2).astype(BF16)
    low, high = inc_low[...].reshape(6 * PAD, 128), inc_high[...].reshape(6 * PAD, 128)
    high = jnp.where((iota(high.shape, 1) == 0) | (iota(high.shape, 1) == 127), high, 0.0)
    wide = dot(pieces(jnp.concatenate([low, high], axis=1)), taps_y)
    wide = (wide[: 6 * PAD] + wide[6 * PAD : 12 * PAD] + wide[12 * PAD :]) * (1.0 / 60.0)
    along[...] = wide.reshape(6, PAD, 256)

    out_row, n = iota((128, 48), 0), iota((128, 48), 1)
    off = (out_row & 15) - 4 * ((n >> 3) - 1)
    taps_x = jnp.where((n & 7) == (out_row >> 4), tap(off, 4), 0.0).astype(BF16)
    taps_x = jnp.concatenate([taps_x] * 3, axis=1)
    copies = []
    for g in range(GROUPS):
        count = min(8, PLANES - 8 * g)
        block = dot(taps_x, pieces(along[:, 8 * g : 8 * g + 8, :].reshape(48, 256)))
        fine[8 * g : 8 * g + 8] = block.reshape(8, 16, 256)
        planes = pl.ds(8 * g, count)
        copies.append(pltpu.make_async_copy(fine.at[planes], fine_hbm.at[planes], sems.at[g]))
        copies[-1].start()
    for i in range(4):
        control[:, i, :] = ctl[i, :PLANES, :]
    for copy in copies:
        copy.wait()


def per_device(
    nx, ny, innovation, area, spread_sd, smooth_coef, obs_column, obs_weight, obs_precision, obs_live
):
    vmem, anywhere = pl.BlockSpec(memory_space=pltpu.VMEM), pl.BlockSpec(memory_space=pl.ANY)
    dma = pltpu.SemaphoreType.DMA
    inc_low, inc_high, ctl = pl.pallas_call(
        functools.partial(solve, nx, ny),
        out_shape=[
            jax.ShapeDtypeStruct((6, PAD, 128), F32),
            jax.ShapeDtypeStruct((6, PAD, 128), F32),
            jax.ShapeDtypeStruct((4, PAD, 128), F32),
        ],
        in_specs=[anywhere, anywhere, anywhere, vmem, vmem, anywhere, vmem, vmem],
        out_specs=[vmem, vmem, vmem],
        scratch_shapes=[
            pltpu.VMEM((PAD, 16, 256), F32),
            pltpu.VMEM((16, 256), F32),
            pltpu.VMEM((PLANES, 4, 128), F32),
            pltpu.VMEM((4, PAD, 128), F32),
            pltpu.VMEM((PLANES, 1024), F32),
            pltpu.VMEM((PAD, 128), F32),
            pltpu.VMEM((PAD, 128), F32),
            pltpu.VMEM((512, 1024), BF16),
            pltpu.VMEM((1024, 512), BF16),
            pltpu.VMEM((256, 256), BF16),
            pltpu.VMEM((6, PAD, 256), F32),
            pltpu.VMEM((6, PAD, 128), F32),
            pltpu.VMEM((6, PAD, 128), F32),
            pltpu.VMEM((2, PAD, 128), F32),
            pltpu.VMEM((3, 12, PAD, 128), F32),
            pltpu.VMEM((5, PAD, 128), F32),
            pltpu.VMEM((5, 6, PAD, 128), F32),
            pltpu.VMEM((3, 8, PAD, 128), F32),
            pltpu.VMEM((3, 8, PAD, 128), F32),
            pltpu.VMEM((8, PAD, 128), F32),
            pltpu.VMEM((8, PAD, 128), F32),
            pltpu.VMEM((6, 3, PAD, 128), F32),
            pltpu.VMEM((MPAD, 512), F32),
            pltpu.VMEM((3 * MPAD, 1024), BF16),
            pltpu.VMEM((3, 2, 128), F32),
            pltpu.VMEM((3, 2, 128), F32),
            pltpu.VMEM((3, ny, 2, 128), F32),
            pltpu.VMEM((3, nx, 2, 128), F32),
            dma((4,)),
            dma((5, 2)),
            dma((5, 2)),
            dma((5, 6)),
            dma((5, 6)),
            dma((3,)),
            dma((3,)),
            dma((3,)),
            dma((3,)),
        ],
        compiler_params=pltpu.CompilerParams(
            collective_id=0, has_side_effects=True, vmem_limit_bytes=40 << 20
        ),
        name="solve",
    )(
        innovation,
        area,
        spread_sd,
        smooth_coef.reshape(1, PLANES),
        obs_column.reshape(8, 128),
        obs_weight,
        obs_precision.reshape(8, 128),
        obs_live.reshape(8, 128),
    )
    return pl.pallas_call(
        finish,
        out_shape=[
            jax.ShapeDtypeStruct((PLANES, 16, 256), F32),
            jax.ShapeDtypeStruct((PLANES, 4, 128), F32),
        ],
        in_specs=[vmem, vmem, vmem],
        out_specs=[anywhere, vmem],
        scratch_shapes=[
            pltpu.VMEM((6, PAD, 256), F32),
            pltpu.VMEM((PAD, 16, 256), F32),
            dma((GROUPS,)),
        ],
        compiler_params=pltpu.CompilerParams(vmem_limit_bytes=24 << 20),
        name="finish",
    )(inc_low, inc_high, ctl)


def solution(mesh):
    nx, ny = mesh.shape["gx"], mesh.shape["gy"]
    return jax.shard_map(
        functools.partial(per_device, nx, ny),
        mesh=mesh,
        in_specs=(
            P(None, "gx", "gy"),
            P("gx", "gy"),
            P(None, "gx", "gy"),
            P(),
            P(("gx", "gy")),
            P(None, ("gx", "gy")),
            P(("gx", "gy")),
            P(("gx", "gy")),
        ),
        out_specs=(P(None, "gx", "gy"), P(None, "gx", "gy")),
        check_vma=False,
    )
```

```python
import functools

import jax
import jax.numpy as jnp
from jax import lax
from jax.experimental import pallas as pl
from jax.experimental.pallas import tpu as pltpu
from jax.sharding import PartitionSpec as P

F32 = jnp.float32
BF16 = jnp.bfloat16
MESH = pl.DeviceIdType.MESH
PLANES = 68
PAD = 72
MPAD = 80
GROUPS = PAD // 8
SIDES = [(sx, sy) for sx in (-1, 0, 1) for sy in (-1, 1)]


def pieces(x):
    high = x.astype(BF16)
    rest = x - high.astype(F32)
    middle = rest.astype(BF16)
    low = (rest - middle.astype(F32)).astype(BF16)
    return jnp.concatenate([high, middle, low], axis=0)


def dot(a, b):
    return jnp.dot(a, b, preferred_element_type=F32)


def iota(shape, dim):
    return lax.broadcasted_iota(jnp.int32, shape, dim)


def tap(offset, ratio):
    inner = (offset >= 0) & (offset < ratio)
    ends = (offset == -1) | (offset == ratio)
    return jnp.where(inner, 2.0, jnp.where(ends, 1.0, 0.0))


def coarse_lane(lane):
    return jnp.where(lane == 255, -1, lane)


def roll(x, shift):
    return pltpu.roll(x, shift % 128, x.ndim - 1)


def beside(low, high, lane):
    low_up, low_down = roll(low, 1), roll(low, 127)
    high_up, high_down = roll(high, 1), roll(high, 127)
    first, last = lane == 0, lane == 127
    of_low = jnp.where(first, high_up, low_up) + jnp.where(last, high_down, low_down)
    of_high = jnp.where(first, low_up, high_up) + jnp.where(last, low_down, high_down)
    return of_low, of_high


def solve(
    nx,
    ny,
    inn_hbm,
    area_hbm,
    sd_hbm,
    coef_hbm,
    col_hbm,
    weight_hbm,
    prec_hbm,
    live_hbm,
    inc_low,
    inc_high,
    ctl,
    inn,
    area,
    sd_in,
    sd,
    weight,
    coef_ref,
    col_ref,
    prec_ref,
    live_ref,
    coef_a,
    coef_b,
    pick,
    place,
    taps_y,
    along,
    rest_low,
    rest_high,
    rim_in,
    field,
    packed,
    packed_in,
    res_low,
    res_high,
    dir_low,
    dir_high,
    ured,
    gathered,
    scaled,
    msg_a,
    msg_b,
    slots_a,
    slots_b,
    in_sems,
    x_send,
    x_recv,
    p_send,
    p_recv,
    a_send,
    a_recv,
    b_send,
    b_recv,
):
    gx, gy = lax.axis_index("gx"), lax.axis_index("gy")

    def at(dx, dy):
        return (lax.rem(gx + dx + nx, nx), lax.rem(gy + dy + ny, ny))

    loads = [
        pltpu.make_async_copy(inn_hbm, inn.at[pl.ds(0, PLANES)], in_sems.at[0]),
        pltpu.make_async_copy(area_hbm, area, in_sems.at[1]),
        pltpu.make_async_copy(sd_hbm, sd_in, in_sems.at[2]),
        pltpu.make_async_copy(weight_hbm, weight, in_sems.at[3]),
        pltpu.make_async_copy(coef_hbm, coef_ref, in_sems.at[4]),
        pltpu.make_async_copy(col_hbm, col_ref, in_sems.at[5]),
        pltpu.make_async_copy(prec_hbm, prec_ref, in_sems.at[6]),
        pltpu.make_async_copy(live_hbm, live_ref, in_sems.at[7]),
    ]
    for load in loads:
        load.start()

    barrier = pltpu.get_barrier_semaphore()
    partners = [at(0, o) for o in range(1, ny)] + [at(o, 0) for o in range(1, nx)]
    partners += [at(dx, dy) for dx in (-1, 1) for dy in (-1, 1)]
    for partner in partners:
        pl.semaphore_signal(barrier, inc=1, device_id=partner, device_id_type=MESH)

    lane8 = iota((8, 128), 1)
    left_ok, right_ok = gx > 0, gx < nx - 1
    low_ok, high_ok = gy > 0, gy < ny - 1
    low_f, high_f = jnp.where(low_ok, 1.0, 0.0), jnp.where(high_ok, 1.0, 0.0)
    edge_f = jnp.where(lane8 < 64, high_f, low_f)
    left_f, right_f = jnp.where(left_ok, 1.0, 0.0), jnp.where(right_ok, 1.0, 0.0)

    def rows(g):
        return pl.ds(8 * g, 8)

    def pack(e, parts, width, block, offset):
        per = 128 // block
        for v in range(-(-GROUPS // per)):
            value = jnp.zeros((8, 128), F32)
            for g in range(per * v, min(per * v + per, GROUPS)):
                for n, part in enumerate(parts[g]):
                    first = block * (g % per) + width * n
                    mine = (lane8 >= first) & (lane8 < first + width)
                    value = jnp.where(mine, roll(part, first + offset), value)
            packed[e, rows(v), :] = value

    inn[PLANES:] = jnp.zeros((PAD - PLANES, 16, 256), F32)
    gathered[PAD:] = jnp.zeros((MPAD - PAD, 512), F32)
    out_row, in_row = iota((48, 384), 0), iota((48, 384), 1) & 127
    same = (out_row & 7) == (in_row >> 4)
    off = (in_row & 15) - 4 * ((out_row >> 3) - 1)
    taps_x = jnp.where(same, tap(off, 4), 0.0).astype(BF16)
    taps_y[...] = tap(iota((256, 256), 0) - 2 * coarse_lane(iota((256, 256), 1)), 2).astype(BF16)

    loads[0].wait()
    loads[1].wait()

    def restrict_x(g, carry):
        at_g = pl.ds(pl.multiple_of(g * 8, 8), 8)
        block = (inn[at_g] * area[...][None]).reshape(128, 256)
        along[:, at_g, :] = dot(taps_x, pieces(block)).reshape(6, 8, 256)
        return carry

    lax.fori_loop(0, GROUPS, restrict_x, 0, unroll=3)
    part = dot(pieces(along[...].reshape(6 * PAD, 256)), taps_y[...])
    part = (part[: 6 * PAD] + part[6 * PAD : 12 * PAD] + part[12 * PAD :]) * (1.0 / 60.0)
    rest_low[...] = part[:, :128].reshape(6, PAD, 128)
    rest_high[...] = part[:, 128:].reshape(6, PAD, 128)

    pack(0, [[rest_high[r, rows(g), :] for r in range(6)] for g in range(GROUPS)], 2, 16, 1)

    pl.semaphore_wait(barrier, len(partners))

    def remote(source, target, send, recv, device):
        copy = pltpu.make_async_remote_copy(
            src_ref=source,
            dst_ref=target,
            send_sem=send,
            recv_sem=recv,
            device_id=device,
            device_id_type=MESH,
        )
        copy.start()
        return copy

    sent = []

    def exchange(e, to_left, at_right, to_right, at_left):
        used = 16 if e == 0 else 24
        copies = [
            remote(to_left, at_right, x_send.at[e, 0], x_recv.at[e, 1], at(-1, 0)),
            remote(to_right, at_left, x_send.at[e, 1], x_recv.at[e, 0], at(1, 0)),
        ]
        for n, (sx, sy) in enumerate(SIDES):
            copies.append(
                remote(
                    packed.at[e, pl.ds(0, used)],
                    packed_in.at[e, n, pl.ds(0, used)],
                    p_send.at[e, n],
                    p_recv.at[e, n],
                    at(-sx, -sy),
                )
            )
        sent.extend(copies)
        return copies

    def arrived(copies):
        for copy in copies:
            copy.wait_recv()

    def sides(e, count, above):
        result = []
        for sx, ok in ((-1, left_ok), (0, None), (1, right_ok)):
            n = 2 * (sx + 1)
            inside = jnp.where(above, high_f, low_f)
            if ok is not None:
                inside = inside * jnp.where(ok, 1.0, 0.0)
            result.append(
                [
                    jnp.where(
                        inside > 0.5,
                        jnp.where(above, packed_in[e, n + 1, rows(v), :], packed_in[e, n, rows(v), :]),
                        0.0,
                    )
                    for v in range(count)
                ]
            )
        return result

    copies = exchange(0, rest_low.at[0], rim_in.at[1], rest_low.at[5], rim_in.at[0])

    for load in loads[2:]:
        load.wait()
    diagonal = iota((PAD, PLANES), 0) == iota((PAD, PLANES), 1)
    coef = jnp.sum(
        jnp.where(diagonal, jnp.broadcast_to(coef_ref[...], (PAD, PLANES)), 0.0),
        axis=1,
        keepdims=True,
    )
    coef_b[...] = jnp.broadcast_to(coef, (PAD, 128))
    coef_a[...] = jnp.broadcast_to(1.0 - 4.0 * coef, (PAD, 128))
    for i in range(4):
        sd[i, :PLANES] = sd_in[:, i, :]
        sd[i, PLANES:] = jnp.zeros((PAD - PLANES, 128), F32)
    cols = col_ref[...]
    cols_t = jnp.transpose(jnp.concatenate([cols.astype(F32), jnp.zeros((120, 128), F32)], axis=0))
    column = iota((512, 128), 0)
    for a in range(8):
        k = pl.ds(128 * a, 128)
        pick[:, k] = jnp.where(column == cols[a : a + 1], 1.0, 0.0).astype(BF16)
        of_slot = jnp.broadcast_to(cols_t[:, a : a + 1], (128, 512))
        place[k, :] = jnp.where(of_slot == iota((128, 512), 1).astype(F32), 1.0, 0.0).astype(BF16)
    obs_scale = prec_ref[...] * live_ref[...].astype(F32)

    arrived(copies)

    rim = sides(0, 2, (lane8 & 1) == 0)
    ends = (lane8 == 0) | (lane8 == 127)
    own = [[] for g in range(GROUPS)]
    for g in range(GROUPS):
        v, first = g // 8, 16 * (g % 8) + 1
        for i in range(4):
            value = rest_low[i + 1, rows(g), :]
            tails = roll(rim[1][v], -(first + 2 * (i + 1)))
            if i == 0:
                value = value + rim_in[0, rows(g), :] * left_f
                tails = tails + roll(rim[0][v], -(first + 10))
            if i == 3:
                value = value + rim_in[1, rows(g), :] * right_f
                tails = tails + roll(rim[2][v], -first)
            value = sd[i, rows(g), :] * (value + jnp.where(ends, tails, 0.0))
            field[0, 4 + i, rows(g), :] = value
            own[g].append(value)

    def pack_and_send(e, parts):
        pack(1 + e, parts, 8, 32, 4)
        own = field.at[e, pl.ds(4, 4)]
        return exchange(1 + e, own, field.at[e, pl.ds(8, 4)], own, field.at[e, pl.ds(0, 4)])

    def smooth(rows, first, coefs):
        result = []
        for n in range(1, len(rows) - 1):
            i = first + n
            a, b, a_high, b_high = coefs[0 if i < 0 else 1 if i < 4 else 2]
            (low, high), before, after = rows[n], rows[n - 1], rows[n + 1]
            of_low, of_high = beside(low, high, lane8)
            of_low = of_low + before[0] + after[0]
            of_high = of_high + before[1] + after[1]
            result.append((a * low + b * of_low, a_high * high + b_high * of_high))
        return result

    def smooth_step(e, alpha, beta):
        tails = sides(1 + e, 3, (lane8 & 4) == 4)
        norm = jnp.zeros((8, 128), F32)
        for g in range(GROUPS):
            at_g = rows(g)
            lines = []
            for r in range(12):
                low = field[e, r, at_g, :]
                if r < 4:
                    low = jnp.where(left_f > 0.5, low, 0.0)
                if r >= 8:
                    low = jnp.where(right_f > 0.5, low, 0.0)
                shift = 32 * (g % 4) + 8 * (r % 4) + 4
                lines.append((low, roll(tails[r // 4][g // 4], -shift)))
            a, b = coef_a[at_g, :], coef_b[at_g, :]
            coefs = [
                (a * f, b * f, a * f * edge_f, b * f * edge_f) for f in (left_f, F32(1.0), right_f)
            ]
            lines = smooth(smooth(lines, -4, coefs), -3, coefs)
            values = []
            for q, (low, high) in enumerate(lines):
                if e > 0:
                    old_low, old_high = res_low[e - 1, q, at_g, :], res_high[e - 1, q, at_g, :]
                    low, high = low + old_low, high + old_high
                    if e > 1:
                        low = low + beta * dir_low[q, at_g, :]
                        high = high + beta * dir_high[q, at_g, :]
                    else:
                        dir_low[q, at_g, :] = low
                        dir_high[q, at_g, :] = high
                    low, high = old_low - alpha * low, old_high - alpha * high
                res_low[e, q, at_g, :] = low
                res_high[e, q, at_g, :] = high
                values.append((low, high))
                if 2 <= q < 6:
                    norm = norm + low * low
            values = smooth(smooth(values, -2, coefs), -1, coefs)
            for i, (low, _) in enumerate(values):
                pushed = sd[i, at_g, :] * low
                ured[1 + i, e, at_g, :] = pushed
                gathered[at_g, pl.ds(128 * i, 128)] = pushed
        return norm

    def observe(e, norm):
        left = pieces(gathered[...])
        total = jnp.zeros((1, 128), F32)
        live = iota((PLANES, 256), 0) >= 0
        for n in range(4):
            k = pl.ds(256 * n, 256)
            taken = dot(left, pick[:, k])
            taken = taken[:MPAD] + taken[MPAD : 2 * MPAD] + taken[2 * MPAD :]
            w = weight[:, k]
            seen = jnp.sum(w * taken[:PLANES], axis=0, keepdims=True)
            scale = jnp.concatenate(
                [obs_scale[2 * n : 2 * n + 1], obs_scale[2 * n + 1 : 2 * n + 2]], axis=1
            )
            value = scale * seen
            square = value * seen
            total = total + square[:, :128] + square[:, 128:]
            if e < 2:
                back = jnp.concatenate([w * value, jnp.zeros((MPAD - PLANES, 256), F32)], axis=0)
                scaled[:, k] = pieces(back)
        msg_a[e] = jnp.concatenate([jnp.sum(norm, axis=0, keepdims=True), total], axis=0)

    def put_back(e):
        own = [[] for g in range(GROUPS)]
        for h in range(2):
            value = dot(scaled[...], place[:, 256 * h : 256 * h + 256])
            value = value[:PAD] + value[MPAD : MPAD + PAD] + value[2 * MPAD : 2 * MPAD + PAD]
            for i in (2 * h, 2 * h + 1):
                row = sd[i] * value[:, 128 * (i % 2) : 128 * (i % 2) + 128]
                field[e, 4 + i] = row
                for g in range(GROUPS):
                    own[g].append(row[8 * g : 8 * g + 8])
        return own

    def reduce_start(k, msg, slots, send, recv, count, mine, partner):
        slots[k, mine] = msg[k]
        for o in range(1, count):
            remote(msg.at[k], slots.at[k, mine], send.at[k], recv.at[k], partner(o))

    def reduce_end(k, slots, send, recv, count, partner):
        several = slots.at[k, pl.ds(0, count - 1)]
        whole = pltpu.make_async_remote_copy(
            src_ref=several,
            dst_ref=several,
            send_sem=send.at[k],
            recv_sem=recv.at[k],
            device_id=partner(1),
            device_id_type=MESH,
        )
        whole.wait_recv()
        whole.wait_send()
        total = slots[k, 0]
        for o in range(1, count):
            total = total + slots[k, o]
        return total

    def start_a(k):
        reduce_start(k, msg_a, slots_a, a_send, a_recv, ny, gy, lambda o: at(0, o))

    def turn(k):
        msg_b[k] = reduce_end(k, slots_a, a_send, a_recv, ny, lambda o: at(0, o))
        reduce_start(k, msg_b, slots_b, b_send, b_recv, nx, gx, lambda o: at(o, 0))

    def end_b(k):
        total = reduce_end(k, slots_b, b_send, b_recv, nx, lambda o: at(o, 0))
        total = jnp.sum(total, axis=1, keepdims=True)
        gamma = jnp.broadcast_to(total[0:1], (8, 128))
        return gamma, gamma + jnp.broadcast_to(total[1:2], (8, 128))

    copies = pack_and_send(0, own)
    arrived(copies)
    norm = smooth_step(0, None, None)
    observe(0, norm)
    start_a(0)
    own = put_back(1)
    copies = pack_and_send(1, own)
    turn(0)
    arrived(copies)
    gamma0, delta0 = end_b(0)
    alpha0 = gamma0 / delta0

    norm = smooth_step(1, alpha0, None)
    observe(1, norm)
    start_a(1)
    own = put_back(2)
    copies = pack_and_send(2, own)
    turn(1)
    arrived(copies)
    gamma1, delta1 = end_b(1)
    beta1 = gamma1 / gamma0
    alpha1 = gamma1 / (delta1 - beta1 * gamma1 / alpha0)

    norm = smooth_step(2, alpha1, beta1)
    observe(2, norm)
    start_a(2)

    rims = [
        [ured[1 + i, v, rows(g), :] for v in range(3) for i in range(4)] for g in range(GROUPS)
    ]
    pack(4, rims, 2, 32, 1)
    copies = exchange(4, ured.at[1], ured.at[5], ured.at[4], ured.at[0])
    turn(2)
    arrived(copies)
    gamma2, delta2 = end_b(2)
    beta2 = gamma2 / gamma1
    alpha2 = gamma2 / (delta2 - beta2 * gamma2 / alpha1)
    parts = [alpha0 + beta1 * (alpha1 + alpha2 * beta2), alpha1 + alpha2 * beta2, alpha2]

    block = lane8 & 31
    of_lane = jnp.where(block < 8, parts[0], jnp.where(block < 16, parts[1], parts[2]))
    tails = []
    for arrays in sides(4, 3, (lane8 & 1) == 1):
        tails.append([])
        for value in arrays:
            value = value * of_lane
            tails[-1].append(value + roll(value, -8) + roll(value, -16))
    for g in range(GROUPS):
        at_g = rows(g)
        for i in range(4):
            ctl[i, at_g, :] = (
                parts[0] * res_low[0, 2 + i, at_g, :]
                + parts[1] * res_low[1, 2 + i, at_g, :]
                + parts[2] * res_low[2, 2 + i, at_g, :]
            )
        for r in range(6):
            value = (
                parts[0] * ured[r, 0, at_g, :]
                + parts[1] * ured[r, 1, at_g, :]
                + parts[2] * ured[r, 2, at_g, :]
            )
            if r == 0:
                value = jnp.where(left_f > 0.5, value, 0.0)
            if r == 5:
                value = jnp.where(right_f > 0.5, value, 0.0)
            inc_low[r, at_g, :] = value
            sx = 0 if r == 0 else 2 if r == 5 else 1
            shift = 32 * (g % 4) + 2 * ((r - 1) % 4) + 1
            inc_high[r, at_g, :] = roll(tails[sx][g // 4], -shift)
    for copy in sent:
        copy.wait_send()


def finish(inc_low, inc_high, ctl, fine_hbm, control, along, fine, sems):
    lane, row = iota((256, 256), 0), iota((256, 256), 1)
    taps_y = tap(row - 2 * coarse_lane(lane), 2).astype(BF16)
    low, high = inc_low[...].reshape(6 * PAD, 128), inc_high[...].reshape(6 * PAD, 128)
    high = jnp.where((iota(high.shape, 1) == 0) | (iota(high.shape, 1) == 127), high, 0.0)
    wide = dot(pieces(jnp.concatenate([low, high], axis=1)), taps_y)
    wide = (wide[: 6 * PAD] + wide[6 * PAD : 12 * PAD] + wide[12 * PAD :]) * (1.0 / 60.0)
    along[...] = wide.reshape(6, PAD, 256)

    out_row, n = iota((128, 48), 0), iota((128, 48), 1)
    off = (out_row & 15) - 4 * ((n >> 3) - 1)
    taps_x = jnp.where((n & 7) == (out_row >> 4), tap(off, 4), 0.0).astype(BF16)
    taps_x = jnp.concatenate([taps_x] * 3, axis=1)
    copies = []
    for g in range(GROUPS):
        count = min(8, PLANES - 8 * g)
        block = dot(taps_x, pieces(along[:, 8 * g : 8 * g + 8, :].reshape(48, 256)))
        fine[8 * g : 8 * g + 8] = block.reshape(8, 16, 256)
        planes = pl.ds(8 * g, count)
        copies.append(pltpu.make_async_copy(fine.at[planes], fine_hbm.at[planes], sems.at[g]))
        copies[-1].start()
    for i in range(4):
        control[:, i, :] = ctl[i, :PLANES, :]
    for copy in copies:
        copy.wait()


def per_device(
    nx, ny, innovation, area, spread_sd, smooth_coef, obs_column, obs_weight, obs_precision, obs_live
):
    vmem, anywhere = pl.BlockSpec(memory_space=pltpu.VMEM), pl.BlockSpec(memory_space=pl.ANY)
    dma = pltpu.SemaphoreType.DMA
    inc_low, inc_high, ctl = pl.pallas_call(
        functools.partial(solve, nx, ny),
        out_shape=[
            jax.ShapeDtypeStruct((6, PAD, 128), F32),
            jax.ShapeDtypeStruct((6, PAD, 128), F32),
            jax.ShapeDtypeStruct((4, PAD, 128), F32),
        ],
        in_specs=[pl.BlockSpec(memory_space=pltpu.HBM)] * 8,
        out_specs=[vmem, vmem, vmem],
        scratch_shapes=[
            pltpu.VMEM((PAD, 16, 256), F32),
            pltpu.VMEM((16, 256), F32),
            pltpu.VMEM((PLANES, 4, 128), F32),
            pltpu.VMEM((4, PAD, 128), F32),
            pltpu.VMEM((PLANES, 1024), F32),
            pltpu.VMEM((1, PLANES), F32),
            pltpu.VMEM((8, 128), jnp.int32),
            pltpu.VMEM((8, 128), F32),
            pltpu.VMEM((8, 128), jnp.int32),
            pltpu.VMEM((PAD, 128), F32),
            pltpu.VMEM((PAD, 128), F32),
            pltpu.VMEM((512, 1024), BF16),
            pltpu.VMEM((1024, 512), BF16),
            pltpu.VMEM((256, 256), BF16),
            pltpu.VMEM((6, PAD, 256), F32),
            pltpu.VMEM((6, PAD, 128), F32),
            pltpu.VMEM((6, PAD, 128), F32),
            pltpu.VMEM((2, PAD, 128), F32),
            pltpu.VMEM((3, 12, PAD, 128), F32),
            pltpu.VMEM((5, 24, 128), F32),
            pltpu.VMEM((5, 6, 24, 128), F32),
            pltpu.VMEM((3, 8, PAD, 128), F32),
            pltpu.VMEM((3, 8, PAD, 128), F32),
            pltpu.VMEM((8, PAD, 128), F32),
            pltpu.VMEM((8, PAD, 128), F32),
            pltpu.VMEM((6, 3, PAD, 128), F32),
            pltpu.VMEM((MPAD, 512), F32),
            pltpu.VMEM((3 * MPAD, 1024), BF16),
            pltpu.VMEM((3, 2, 128), F32),
            pltpu.VMEM((3, 2, 128), F32),
            pltpu.VMEM((3, ny, 2, 128), F32),
            pltpu.VMEM((3, nx, 2, 128), F32),
            dma((8,)),
            dma((5, 2)),
            dma((5, 2)),
            dma((5, 6)),
            dma((5, 6)),
            dma((3,)),
            dma((3,)),
            dma((3,)),
            dma((3,)),
        ],
        compiler_params=pltpu.CompilerParams(
            collective_id=0, has_side_effects=True, vmem_limit_bytes=40 << 20
        ),
        name="solve",
    )(
        *(
            pltpu.with_memory_space_constraint(operand, pltpu.HBM)
            for operand in (
                innovation,
                area,
                spread_sd,
                smooth_coef.reshape(1, PLANES),
                obs_column.reshape(8, 128),
                obs_weight,
                obs_precision.reshape(8, 128),
                obs_live.reshape(8, 128),
            )
        )
    )
    return pl.pallas_call(
        finish,
        out_shape=[
            jax.ShapeDtypeStruct((PLANES, 16, 256), F32),
            jax.ShapeDtypeStruct((PLANES, 4, 128), F32),
        ],
        in_specs=[vmem, vmem, vmem],
        out_specs=[anywhere, vmem],
        scratch_shapes=[
            pltpu.VMEM((6, PAD, 256), F32),
            pltpu.VMEM((PAD, 16, 256), F32),
            dma((GROUPS,)),
        ],
        compiler_params=pltpu.CompilerParams(vmem_limit_bytes=24 << 20),
        name="finish",
    )(inc_low, inc_high, ctl)


def solution(mesh):
    nx, ny = mesh.shape["gx"], mesh.shape["gy"]
    return jax.shard_map(
        functools.partial(per_device, nx, ny),
        mesh=mesh,
        in_specs=(
            P(None, "gx", "gy"),
            P("gx", "gy"),
            P(None, "gx", "gy"),
            P(),
            P(("gx", "gy")),
            P(None, ("gx", "gy")),
            P(("gx", "gy")),
            P(("gx", "gy")),
        ),
        out_specs=(P(None, "gx", "gy"), P(None, "gx", "gy")),
        check_vma=False,
    )
```

```python
import functools

import jax
import jax.numpy as jnp
from jax import lax
from jax.experimental import pallas as pl
from jax.experimental.pallas import tpu as pltpu
from jax.sharding import PartitionSpec as P

F32 = jnp.float32
BF16 = jnp.bfloat16
MESH = pl.DeviceIdType.MESH
PLANES = 68
PAD = 72
MPAD = 80
GROUPS = PAD // 8
SIDES = [(sx, sy) for sx in (-1, 0, 1) for sy in (-1, 1)]


def pieces(x):
    high = x.astype(BF16)
    rest = x - high.astype(F32)
    middle = rest.astype(BF16)
    low = (rest - middle.astype(F32)).astype(BF16)
    return jnp.concatenate([high, middle, low], axis=0)


def dot(a, b):
    return jnp.dot(a, b, preferred_element_type=F32)


def iota(shape, dim):
    return lax.broadcasted_iota(jnp.int32, shape, dim)


def tap(offset, ratio):
    inner = (offset >= 0) & (offset < ratio)
    ends = (offset == -1) | (offset == ratio)
    return jnp.where(inner, 2.0, jnp.where(ends, 1.0, 0.0))


def coarse_lane(lane):
    return jnp.where(lane == 255, -1, lane)


def roll(x, shift):
    return pltpu.roll(x, shift % 128, x.ndim - 1)


def beside(low, high, lane):
    low_up, low_down = roll(low, 1), roll(low, 127)
    high_up, high_down = roll(high, 1), roll(high, 127)
    first, last = lane == 0, lane == 127
    of_low = jnp.where(first, high_up, low_up) + jnp.where(last, high_down, low_down)
    of_high = jnp.where(first, low_up, high_up) + jnp.where(last, low_down, high_down)
    return of_low, of_high


def solve(
    nx,
    ny,
    inn_hbm,
    area_hbm,
    sd_hbm,
    coef_hbm,
    col_hbm,
    weight_hbm,
    prec_hbm,
    live_hbm,
    fine,
    ctl,
    steps,
    inn,
    area,
    sd_in,
    sd,
    weight,
    coef_ref,
    col_ref,
    prec_ref,
    live_ref,
    coef_a,
    coef_b,
    pick,
    place,
    taps_y,
    along,
    rest_low,
    rest_high,
    rim_in,
    field,
    packed,
    packed_in,
    base_low,
    base_high,
    ured,
    gathered,
    scaled,
    msg_a,
    msg_b,
    slots_a,
    slots_b,
    in_sems,
    x_send,
    x_recv,
    p_send,
    p_recv,
    a_send,
    a_recv,
    b_send,
    b_recv,
):
    gx, gy = lax.axis_index("gx"), lax.axis_index("gy")

    def shifted(here, step, size):
        if step == 0:
            return here
        if size & (size - 1) == 0:
            return (here + (step + size)) & (size - 1)
        return lax.rem(here + (step + size), size)

    def at(dx, dy):
        return (shifted(gx, dx, nx), shifted(gy, dy, ny))

    loads = [
        pltpu.make_async_copy(inn_hbm, inn.at[pl.ds(0, PLANES)], in_sems.at[0]),
        pltpu.make_async_copy(area_hbm, area, in_sems.at[1]),
        pltpu.make_async_copy(sd_hbm, sd_in, in_sems.at[2]),
        pltpu.make_async_copy(weight_hbm, weight, in_sems.at[3]),
        pltpu.make_async_copy(coef_hbm, coef_ref, in_sems.at[4]),
        pltpu.make_async_copy(col_hbm, col_ref, in_sems.at[5]),
        pltpu.make_async_copy(prec_hbm, prec_ref, in_sems.at[6]),
        pltpu.make_async_copy(live_hbm, live_ref, in_sems.at[7]),
    ]
    for load in loads:
        load.start()

    barrier = pltpu.get_barrier_semaphore()
    partners = [at(0, o) for o in range(1, ny)] + [at(o, 0) for o in range(1, nx)]
    partners += [at(dx, dy) for dx in (-1, 1) for dy in (-1, 1)]
    for partner in partners:
        pl.semaphore_signal(barrier, inc=1, device_id=partner, device_id_type=MESH)

    lane8 = iota((8, 128), 1)
    left_ok, right_ok = gx > 0, gx < nx - 1
    low_ok, high_ok = gy > 0, gy < ny - 1
    low_f, high_f = jnp.where(low_ok, 1.0, 0.0), jnp.where(high_ok, 1.0, 0.0)
    edge_f = jnp.where(lane8 < 64, high_f, low_f)
    left_f, right_f = jnp.where(left_ok, 1.0, 0.0), jnp.where(right_ok, 1.0, 0.0)

    def rows(g):
        return pl.ds(8 * g, 8)

    def pack(e, parts, width, block, offset):
        per = 128 // block
        for v in range(-(-GROUPS // per)):
            value = jnp.zeros((8, 128), F32)
            for g in range(per * v, min(per * v + per, GROUPS)):
                for n, part in enumerate(parts[g]):
                    first = block * (g % per) + width * n
                    mine = (lane8 >= first) & (lane8 < first + width)
                    value = jnp.where(mine, roll(part, first + offset), value)
            packed[e, rows(v), :] = value

    inn[PLANES:] = jnp.zeros((PAD - PLANES, 16, 256), F32)
    gathered[PAD:] = jnp.zeros((MPAD - PAD, 512), F32)
    out_row, in_row = iota((48, 384), 0), iota((48, 384), 1) & 127
    same = (out_row & 7) == (in_row >> 4)
    off = (in_row & 15) - 4 * ((out_row >> 3) - 1)
    taps_x = jnp.where(same, tap(off, 4), 0.0).astype(BF16)
    taps_y[...] = tap(iota((256, 256), 0) - 2 * coarse_lane(iota((256, 256), 1)), 2).astype(BF16)

    loads[0].wait()
    loads[1].wait()

    def restrict_x(g, carry):
        at_g = pl.ds(pl.multiple_of(g * 8, 8), 8)
        block = (inn[at_g] * area[...][None]).reshape(128, 256)
        along[:, at_g, :] = dot(taps_x, pieces(block)).reshape(6, 8, 256)
        return carry

    lax.fori_loop(0, GROUPS, restrict_x, 0, unroll=3)
    part = dot(pieces(along[...].reshape(6 * PAD, 256)), taps_y[...])
    part = (part[: 6 * PAD] + part[6 * PAD : 12 * PAD] + part[12 * PAD :]) * (1.0 / 60.0)
    rest_low[...] = part[:, :128].reshape(6, PAD, 128)
    rest_high[...] = part[:, 128:].reshape(6, PAD, 128)

    pack(0, [[rest_high[r, rows(g), :] for r in range(6)] for g in range(GROUPS)], 2, 16, 1)

    pl.semaphore_wait(barrier, len(partners))

    def remote(source, target, send, recv, device):
        copy = pltpu.make_async_remote_copy(
            src_ref=source,
            dst_ref=target,
            send_sem=send,
            recv_sem=recv,
            device_id=device,
            device_id_type=MESH,
        )
        copy.start()
        return copy

    sent = []

    def inside(dx, dy):
        ok = None
        for here, step, size in ((gx, dx, nx), (gy, dy, ny)):
            if step:
                holds = here > 0 if step < 0 else here < size - 1
                ok = holds if ok is None else ok & holds
        return ok

    def send(moves):
        copies = []
        for dx, dy, source, target, send_sem, recv_sem in moves:
            copy = pltpu.make_async_remote_copy(
                src_ref=source,
                dst_ref=target,
                send_sem=send_sem,
                recv_sem=recv_sem,
                device_id=at(dx, dy),
                device_id_type=MESH,
            )
            pl.when(inside(dx, dy))(copy.start)
            copies.append((dx, dy, copy))
        sent.extend(copies)
        return copies

    def row_moves(e, to_left, at_right, to_right, at_left):
        return [
            (-1, 0, to_left, at_right, x_send.at[e, 0], x_recv.at[e, 1]),
            (1, 0, to_right, at_left, x_send.at[e, 1], x_recv.at[e, 0]),
        ]

    def side_moves(e):
        used = pl.ds(0, 16 if e == 0 else 24)
        return [
            (
                -sx,
                -sy,
                packed.at[e, used],
                packed_in.at[e, n, used],
                p_send.at[e, n],
                p_recv.at[e, n],
            )
            for n, (sx, sy) in enumerate(SIDES)
        ]

    def rim_rows(v):
        return row_moves(4 + v, ured.at[1, v], ured.at[5, v], ured.at[4, v], ured.at[0, v])

    def arrived(copies):
        for dx, dy, copy in copies:
            pl.when(inside(-dx, -dy))(copy.wait_recv)

    def sides(e, count, above):
        result = []
        for sx, ok in ((-1, left_ok), (0, None), (1, right_ok)):
            n = 2 * (sx + 1)
            there = jnp.where(above, high_f, low_f)
            if ok is not None:
                there = there * jnp.where(ok, 1.0, 0.0)
            result.append(
                [
                    jnp.where(
                        there > 0.5,
                        jnp.where(above, packed_in[e, n + 1, rows(v), :], packed_in[e, n, rows(v), :]),
                        0.0,
                    )
                    for v in range(count)
                ]
            )
        return result

    copies = send(
        row_moves(0, rest_low.at[0], rim_in.at[1], rest_low.at[5], rim_in.at[0]) + side_moves(0)
    )

    for load in loads[2:]:
        load.wait()
    diagonal = iota((PAD, PLANES), 0) == iota((PAD, PLANES), 1)
    coef = jnp.sum(
        jnp.where(diagonal, jnp.broadcast_to(coef_ref[...], (PAD, PLANES)), 0.0),
        axis=1,
        keepdims=True,
    )
    coef_b[...] = jnp.broadcast_to(coef, (PAD, 128))
    coef_a[...] = jnp.broadcast_to(1.0 - 4.0 * coef, (PAD, 128))
    for i in range(4):
        sd[i, :PLANES] = sd_in[:, i, :]
        sd[i, PLANES:] = jnp.zeros((PAD - PLANES, 128), F32)
    cols = col_ref[...]
    cols_t = jnp.transpose(jnp.concatenate([cols.astype(F32), jnp.zeros((120, 128), F32)], axis=0))
    column = iota((512, 128), 0)
    for a in range(8):
        k = pl.ds(128 * a, 128)
        pick[:, k] = jnp.where(column == cols[a : a + 1], 1.0, 0.0).astype(BF16)
        of_slot = jnp.broadcast_to(cols_t[:, a : a + 1], (128, 512))
        place[k, :] = jnp.where(of_slot == iota((128, 512), 1).astype(F32), 1.0, 0.0).astype(BF16)
    obs_scale = prec_ref[...] * live_ref[...].astype(F32)

    arrived(copies)

    rim = sides(0, 2, (lane8 & 1) == 0)
    ends = (lane8 == 0) | (lane8 == 127)
    own = [[] for g in range(GROUPS)]
    for g in range(GROUPS):
        v, first = g // 8, 16 * (g % 8) + 1
        for i in range(4):
            value = rest_low[i + 1, rows(g), :]
            tails = roll(rim[1][v], -(first + 2 * (i + 1)))
            if i == 0:
                value = value + jnp.where(left_f > 0.5, rim_in[0, rows(g), :], 0.0)
                tails = tails + roll(rim[0][v], -(first + 10))
            if i == 3:
                value = value + jnp.where(right_f > 0.5, rim_in[1, rows(g), :], 0.0)
                tails = tails + roll(rim[2][v], -first)
            value = sd[i, rows(g), :] * (value + jnp.where(ends, tails, 0.0))
            field[0, 4 + i, rows(g), :] = value
            own[g].append(value)

    def pack_and_send(e, parts):
        pack(1 + e, parts, 8, 32, 4)
        own = field.at[e, pl.ds(4, 4)]
        after, before = field.at[e, pl.ds(8, 4)], field.at[e, pl.ds(0, 4)]
        return send(row_moves(1 + e, own, after, own, before) + side_moves(1 + e))

    def smooth(rows, first, coefs):
        result = []
        for n in range(1, len(rows) - 1):
            i = first + n
            a, b, a_high, b_high = coefs[0 if i < 0 else 1 if i < 4 else 2]
            (low, high), before, after = rows[n], rows[n - 1], rows[n + 1]
            of_low, of_high = beside(low, high, lane8)
            of_low = of_low + before[0] + after[0]
            of_high = of_high + before[1] + after[1]
            result.append((a * low + b * of_low, a_high * high + b_high * of_high))
        return result

    def smooth_step(e, alpha):
        tails = sides(1 + e, 3, (lane8 & 4) == 4)
        for g in range(GROUPS):
            at_g = rows(g)
            lines = []
            for r in range(12):
                low = field[e, r, at_g, :]
                if r < 4:
                    low = jnp.where(left_f > 0.5, low, 0.0)
                if r >= 8:
                    low = jnp.where(right_f > 0.5, low, 0.0)
                shift = 32 * (g % 4) + 8 * (r % 4) + 4
                lines.append((low, roll(tails[r // 4][g // 4], -shift)))
            a, b = coef_a[at_g, :], coef_b[at_g, :]
            coefs = [
                (a * f, b * f, a * f * edge_f, b * f * edge_f) for f in (left_f, F32(1.0), right_f)
            ]
            lines = smooth(smooth(lines, -4, coefs), -3, coefs)
            values = []
            for q, (low, high) in enumerate(lines):
                if e > 0:
                    low, high = low + base_low[0, q, at_g, :], high + base_high[0, q, at_g, :]
                if e > 1:
                    low = low - alpha * base_low[1, q, at_g, :]
                    high = high - alpha * base_high[1, q, at_g, :]
                base_low[e, q, at_g, :] = low
                if e < 2:
                    base_high[e, q, at_g, :] = high
                values.append((low, high))
            values = smooth(smooth(values, -2, coefs), -1, coefs)
            for i, (low, _) in enumerate(values):
                pushed = sd[i, at_g, :] * low
                ured[1 + i, e, at_g, :] = pushed
                gathered[at_g, pl.ds(128 * i, 128)] = pushed

    def observe():
        left = pieces(gathered[...])
        seen = []
        for n in range(4):
            k = pl.ds(256 * n, 256)
            taken = dot(left, pick[:, k])
            taken = taken[:MPAD] + taken[MPAD : 2 * MPAD] + taken[2 * MPAD :]
            seen.append(jnp.sum(weight[:, k] * taken[:PLANES], axis=0, keepdims=True))
        return seen

    def wide(x):
        return jnp.concatenate([x[:1], x[:1]], axis=1)

    def squares(e, seen, norm):
        scaled_seen, total = [], jnp.zeros((1, 128), F32)
        for n in range(4):
            scale = jnp.concatenate(
                [obs_scale[2 * n : 2 * n + 1], obs_scale[2 * n + 1 : 2 * n + 2]], axis=1
            )
            value = scale * seen[n]
            scaled_seen.append(value)
            square = value * seen[n]
            total = total + square[:, :128] + square[:, 128:]
        msg_a[e] = jnp.concatenate([jnp.sum(norm, axis=0, keepdims=True), total], axis=0)
        return scaled_seen

    def scatter(scaled_seen):
        for n in range(4):
            k = pl.ds(256 * n, 256)
            back = weight[:, k] * scaled_seen[n]
            back = jnp.concatenate([back, jnp.zeros((MPAD - PLANES, 256), F32)], axis=0)
            scaled[:, k] = pieces(back)

    def own_norm(factors):
        norm = jnp.zeros((8, 128), F32)
        for g in range(GROUPS):
            for i in range(4):
                value = base_low[0, 2 + i, rows(g), :]
                for v, factor in enumerate(factors):
                    value = value + factor * base_low[1 + v, 2 + i, rows(g), :]
                norm = norm + value * value
        return norm

    def put_back(e):
        own = [[] for g in range(GROUPS)]
        for h in range(2):
            value = dot(scaled[...], place[:, 256 * h : 256 * h + 256])
            value = value[:PAD] + value[MPAD : MPAD + PAD] + value[2 * MPAD : 2 * MPAD + PAD]
            for i in (2 * h, 2 * h + 1):
                row = sd[i] * value[:, 128 * (i % 2) : 128 * (i % 2) + 128]
                field[e, 4 + i] = row
                for g in range(GROUPS):
                    own[g].append(row[8 * g : 8 * g + 8])
        return own

    def reduce_start(k, msg, slots, send_sem, recv_sem, offsets, mine, partner):
        slots[k, mine] = msg[k]
        for o in offsets:
            pltpu.make_async_remote_copy(
                src_ref=msg.at[k],
                dst_ref=slots.at[k, mine],
                send_sem=send_sem.at[k],
                recv_sem=recv_sem.at[k],
                device_id=partner(o),
                device_id_type=MESH,
            ).start()

    def all_of(k, slots, send_sem, recv_sem, count, partner):
        several = slots.at[k, pl.ds(0, count - 1)]
        return pltpu.make_async_remote_copy(
            src_ref=several,
            dst_ref=several,
            send_sem=send_sem.at[k],
            recv_sem=recv_sem.at[k],
            device_id=partner(1),
            device_id_type=MESH,
        )

    def total_of(k, slots, count):
        totals = [slots[k, o] for o in range(count)]
        while len(totals) > 1:
            totals = [sum(totals[n : n + 2]) for n in range(0, len(totals), 2)]
        return totals[0]

    def far_first(size):
        return sorted(range(1, size), key=lambda o: -min(o, size - o))

    def over_y(o):
        return at(0, o)

    def over_x(o):
        return at(o, 0)

    def start_a(k):
        reduce_start(k, msg_a, slots_a, a_send, a_recv, far_first(ny), gy, over_y)

    def turn(k):
        all_of(k, slots_a, a_send, a_recv, ny, over_y).wait_recv()
        msg_b[k] = total_of(k, slots_a, ny)
        reduce_start(k, msg_b, slots_b, b_send, b_recv, far_first(nx), gx, over_x)

    def end_b(k):
        all_of(k, slots_b, b_send, b_recv, nx, over_x).wait_recv()
        total = total_of(k, slots_b, nx)
        total = jnp.sum(total, axis=1, keepdims=True)
        gamma = jnp.broadcast_to(total[0:1], (8, 128))
        return gamma, gamma + jnp.broadcast_to(total[1:2], (8, 128))

    copies = pack_and_send(0, own)
    arrived(copies)
    smooth_step(0, None)
    seen0 = observe()
    values = squares(0, seen0, own_norm([]))
    start_a(0)
    scatter(values)
    own = put_back(1)
    copies = pack_and_send(1, own)
    turn(0)
    arrived(copies)

    rims = send(rim_rows(0))
    smooth_step(1, None)
    seen1 = observe()
    gamma0, delta0 = end_b(0)
    alpha0 = gamma0 / delta0
    seen_r1 = [a - wide(alpha0) * b for a, b in zip(seen0, seen1)]
    values = squares(1, seen_r1, own_norm([-alpha0]))
    start_a(1)
    scatter(values)
    own = put_back(2)
    copies = pack_and_send(2, own)
    turn(1)
    arrived(copies)

    rims += send(rim_rows(1))
    smooth_step(2, alpha0)
    edges = [
        [ured[1 + i, v, rows(g), :] for v in range(3) for i in range(4)] for g in range(GROUPS)
    ]
    pack(4, edges, 2, 32, 1)
    rims += send(rim_rows(2) + side_moves(4))
    seen2 = observe()
    gamma1, delta1 = end_b(1)
    beta1 = gamma1 / gamma0
    alpha1 = gamma1 / (delta1 - beta1 * gamma1 / alpha0)
    seen_r2 = [
        a - wide(alpha1) * (b + wide(beta1) * c) for a, b, c in zip(seen_r1, seen2, seen1)
    ]
    of_r2 = [-alpha0 - alpha1 * beta1, -alpha1]
    squares(2, seen_r2, own_norm(of_r2))
    start_a(2)

    both = 1.0 + beta1
    factors = [
        [alpha0 + alpha1 * both, -alpha1 * alpha0],
        [jnp.ones((8, 128), F32)] + of_r2,
        [both, -alpha0],
    ]
    for g in range(GROUPS):
        for i in range(4):
            for b in range(3):
                ctl[b, i, rows(g), :] = sum(
                    f * base_low[v, 2 + i, rows(g), :] for v, f in enumerate(factors[b])
                )
    arrived(rims)
    tails = sides(4, 3, (lane8 & 1) == 1)
    block = lane8 & 31
    out_row, in_col = iota((128, 48), 0), iota((128, 48), 1)
    off = (out_row & 15) - 4 * ((in_col >> 3) - 1)
    spread_x = jnp.where((in_col & 7) == (out_row >> 4), tap(off, 4), 0.0).astype(BF16)
    spread_x = jnp.concatenate([spread_x] * 3, axis=1)
    spread_y = tap(iota((256, 256), 1) - 2 * coarse_lane(iota((256, 256), 0)), 2).astype(BF16)
    sides_in = (lane8 == 0) | (lane8 == 127)

    def interpolate(b):
        most = factors[b] + [jnp.zeros((8, 128), F32)] * (3 - len(factors[b]))
        of_lane = jnp.where(block < 8, most[0], jnp.where(block < 16, most[1], most[2]))
        ends = []
        for arrays in tails:
            ends.append([])
            for value in arrays:
                value = value * of_lane
                ends[-1].append(value + roll(value, -8) + roll(value, -16))
        for g in range(GROUPS):
            for r in range(6):
                value = sum(f * ured[r, v, rows(g), :] for v, f in enumerate(factors[b]))
                if r == 0:
                    value = jnp.where(left_f > 0.5, value, 0.0)
                if r == 5:
                    value = jnp.where(right_f > 0.5, value, 0.0)
                sx = 0 if r == 0 else 2 if r == 5 else 1
                shift = 32 * (g % 4) + 2 * ((r - 1) % 4) + 1
                end = jnp.where(sides_in, roll(ends[sx][g // 4], -shift), 0.0)
                along[r, rows(g), :] = jnp.concatenate([value, end], axis=1)
        out = dot(pieces(along[...].reshape(6 * PAD, 256)), spread_y)
        out = (out[: 6 * PAD] + out[6 * PAD : 12 * PAD] + out[12 * PAD :]) * (1.0 / 60.0)
        out = out.reshape(6, PAD, 256)
        for g in range(GROUPS):
            part = dot(spread_x, pieces(out[:, 8 * g : 8 * g + 8, :].reshape(48, 256)))
            fine[b, rows(g)] = part.reshape(8, 16, 256)

    interpolate(0)
    turn(2)
    interpolate(1)
    interpolate(2)
    gamma2, delta2 = end_b(2)
    beta2 = gamma2 / gamma1
    alpha2 = gamma2 / (delta2 - beta2 * gamma2 / alpha1)
    steps[0] = alpha2
    steps[1] = alpha2 * beta2

    for dx, dy, copy in sent:
        pl.when(inside(dx, dy))(copy.wait_send)
    for k in range(3):
        all_of(k, slots_a, a_send, a_recv, ny, over_y).wait_send()
        all_of(k, slots_b, b_send, b_recv, nx, over_x).wait_send()


def finish(parts, ctl, steps, fine_hbm, control, fine, sems):
    first, second = steps[0], steps[1]
    first = jnp.concatenate([first, first], axis=1)
    second = jnp.concatenate([second, second], axis=1)
    copies = []
    for g in range(GROUPS):
        count = min(8, PLANES - 8 * g)
        for p in range(8 * g, 8 * g + count):
            for h in range(2):
                at_h = pl.ds(8 * h, 8)
                fine[p, at_h, :] = (
                    parts[0, p, at_h, :] + first * parts[1, p, at_h, :] + second * parts[2, p, at_h, :]
                )
        planes = pl.ds(8 * g, count)
        copies.append(pltpu.make_async_copy(fine.at[planes], fine_hbm.at[planes], sems.at[g]))
        copies[-1].start()
    for i in range(4):
        value = ctl[0, i] + steps[0][:1] * ctl[1, i] + steps[1][:1] * ctl[2, i]
        control[:, i, :] = value[:PLANES]
    for copy in copies:
        copy.wait()


def per_device(
    nx, ny, innovation, area, spread_sd, smooth_coef, obs_column, obs_weight, obs_precision, obs_live
):
    vmem, anywhere = pl.BlockSpec(memory_space=pltpu.VMEM), pl.BlockSpec(memory_space=pl.ANY)
    dma = pltpu.SemaphoreType.DMA
    fine, ctl, steps = pl.pallas_call(
        functools.partial(solve, nx, ny),
        out_shape=[
            jax.ShapeDtypeStruct((3, PAD, 16, 256), F32),
            jax.ShapeDtypeStruct((3, 4, PAD, 128), F32),
            jax.ShapeDtypeStruct((2, 8, 128), F32),
        ],
        in_specs=[pl.BlockSpec(memory_space=pltpu.HBM)] * 8,
        out_specs=[vmem, vmem, vmem],
        scratch_shapes=[
            pltpu.VMEM((PAD, 16, 256), F32),
            pltpu.VMEM((16, 256), F32),
            pltpu.VMEM((PLANES, 4, 128), F32),
            pltpu.VMEM((4, PAD, 128), F32),
            pltpu.VMEM((PLANES, 1024), F32),
            pltpu.VMEM((1, PLANES), F32),
            pltpu.VMEM((8, 128), jnp.int32),
            pltpu.VMEM((8, 128), F32),
            pltpu.VMEM((8, 128), jnp.int32),
            pltpu.VMEM((PAD, 128), F32),
            pltpu.VMEM((PAD, 128), F32),
            pltpu.VMEM((512, 1024), BF16),
            pltpu.VMEM((1024, 512), BF16),
            pltpu.VMEM((256, 256), BF16),
            pltpu.VMEM((6, PAD, 256), F32),
            pltpu.VMEM((6, PAD, 128), F32),
            pltpu.VMEM((6, PAD, 128), F32),
            pltpu.VMEM((2, PAD, 128), F32),
            pltpu.VMEM((3, 12, PAD, 128), F32),
            pltpu.VMEM((5, 24, 128), F32),
            pltpu.VMEM((5, 6, 24, 128), F32),
            pltpu.VMEM((3, 8, PAD, 128), F32),
            pltpu.VMEM((2, 8, PAD, 128), F32),
            pltpu.VMEM((6, 3, PAD, 128), F32),
            pltpu.VMEM((MPAD, 512), F32),
            pltpu.VMEM((3 * MPAD, 1024), BF16),
            pltpu.VMEM((3, 2, 128), F32),
            pltpu.VMEM((3, 2, 128), F32),
            pltpu.VMEM((3, ny, 2, 128), F32),
            pltpu.VMEM((3, nx, 2, 128), F32),
            dma((8,)),
            dma((7, 2)),
            dma((7, 2)),
            dma((5, 6)),
            dma((5, 6)),
            dma((3,)),
            dma((3,)),
            dma((3,)),
            dma((3,)),
        ],
        compiler_params=pltpu.CompilerParams(
            collective_id=0, has_side_effects=True, vmem_limit_bytes=40 << 20
        ),
        name="solve",
    )(
        *(
            pltpu.with_memory_space_constraint(operand, pltpu.HBM)
            for operand in (
                innovation,
                area,
                spread_sd,
                smooth_coef.reshape(1, PLANES),
                obs_column.reshape(8, 128),
                obs_weight,
                obs_precision.reshape(8, 128),
                obs_live.reshape(8, 128),
            )
        )
    )
    return pl.pallas_call(
        finish,
        out_shape=[
            jax.ShapeDtypeStruct((PLANES, 16, 256), F32),
            jax.ShapeDtypeStruct((PLANES, 4, 128), F32),
        ],
        in_specs=[vmem, vmem, vmem],
        out_specs=[anywhere, vmem],
        scratch_shapes=[
            pltpu.VMEM((PAD, 16, 256), F32),
            dma((GROUPS,)),
        ],
        compiler_params=pltpu.CompilerParams(vmem_limit_bytes=24 << 20),
        name="finish",
    )(fine, ctl, steps)


def solution(mesh):
    nx, ny = mesh.shape["gx"], mesh.shape["gy"]
    return jax.shard_map(
        functools.partial(per_device, nx, ny),
        mesh=mesh,
        in_specs=(
            P(None, "gx", "gy"),
            P("gx", "gy"),
            P(None, "gx", "gy"),
            P(),
            P(("gx", "gy")),
            P(None, ("gx", "gy")),
            P(("gx", "gy")),
            P(("gx", "gy")),
        ),
        out_specs=(P(None, "gx", "gy"), P(None, "gx", "gy")),
        check_vma=False,
    )
```

```python
import functools

import jax
import jax.numpy as jnp
from jax import lax
from jax.experimental import pallas as pl
from jax.experimental.pallas import tpu as pltpu
from jax.sharding import PartitionSpec as P

F32 = jnp.float32
BF16 = jnp.bfloat16
MESH = pl.DeviceIdType.MESH
PLANES = 68
PAD = 72
MPAD = 80
GROUPS = PAD // 8
SCALE = 1.0 / 256.0
PAIRS = [(0, 0), (0, 1), (0, 2), (1, 1), (1, 2), (2, 2)]
SIDES = [(sx, sy) for sx in (-1, 0, 1) for sy in (-1, 1)]


def pieces(x):
    high = x.astype(BF16)
    rest = x - high.astype(F32)
    middle = rest.astype(BF16)
    low = (rest - middle.astype(F32)).astype(BF16)
    return jnp.concatenate([high, middle, low], axis=0)


def dot(a, b):
    return jnp.dot(a, b, preferred_element_type=F32)


def iota(shape, dim):
    return lax.broadcasted_iota(jnp.int32, shape, dim)


def tap(offset, ratio):
    inner = (offset >= 0) & (offset < ratio)
    ends = (offset == -1) | (offset == ratio)
    return jnp.where(inner, 2.0, jnp.where(ends, 1.0, 0.0))


def coarse_lane(lane):
    return jnp.where(lane == 255, -1, lane)


def roll(x, shift):
    return pltpu.roll(x, shift % 128, x.ndim - 1)


def beside(low, high, lane):
    low_up, low_down = roll(low, 1), roll(low, 127)
    high_up, high_down = roll(high, 1), roll(high, 127)
    first, last = lane == 0, lane == 127
    of_low = jnp.where(first, high_up, low_up) + jnp.where(last, high_down, low_down)
    of_high = jnp.where(first, low_up, high_up) + jnp.where(last, low_down, high_down)
    return of_low, of_high


def solve(
    nx,
    ny,
    inn_hbm,
    area_hbm,
    sd_hbm,
    coef_hbm,
    col_hbm,
    weight_hbm,
    prec_hbm,
    live_hbm,
    fine,
    ctl,
    steps,
    inn,
    area,
    sd_in,
    sd,
    weight,
    coef_ref,
    col_ref,
    prec_ref,
    live_ref,
    coef_a,
    coef_b,
    pick,
    place,
    taps_y,
    along,
    rest_low,
    rest_high,
    rim_in,
    field,
    packed,
    packed_in,
    base,
    ured,
    gathered,
    scaled,
    msg_a,
    msg_b,
    slots_a,
    slots_b,
    in_sems,
    x_send,
    x_recv,
    p_send,
    p_recv,
    a_send,
    a_recv,
    b_send,
    b_recv,
):
    gx, gy = lax.axis_index("gx"), lax.axis_index("gy")

    def shifted(here, step, size):
        if step == 0:
            return here
        if size & (size - 1) == 0:
            return (here + (step + size)) & (size - 1)
        return lax.rem(here + (step + size), size)

    def at(dx, dy):
        return (shifted(gx, dx, nx), shifted(gy, dy, ny))

    loads = [
        pltpu.make_async_copy(inn_hbm, inn.at[pl.ds(0, PLANES)], in_sems.at[0]),
        pltpu.make_async_copy(area_hbm, area, in_sems.at[1]),
        pltpu.make_async_copy(sd_hbm, sd_in, in_sems.at[2]),
        pltpu.make_async_copy(weight_hbm, weight, in_sems.at[3]),
        pltpu.make_async_copy(coef_hbm, coef_ref, in_sems.at[4]),
        pltpu.make_async_copy(col_hbm, col_ref, in_sems.at[5]),
        pltpu.make_async_copy(prec_hbm, prec_ref, in_sems.at[6]),
        pltpu.make_async_copy(live_hbm, live_ref, in_sems.at[7]),
    ]
    for load in loads:
        load.start()

    barrier = pltpu.get_barrier_semaphore()
    partners = [at(0, o) for o in range(1, ny)] + [at(o, 0) for o in range(1, nx)]
    partners += [at(dx, dy) for dx in (-1, 1) for dy in (-1, 1)]
    for partner in partners:
        pl.semaphore_signal(barrier, inc=1, device_id=partner, device_id_type=MESH)

    lane8 = iota((8, 128), 1)
    left_ok, right_ok = gx > 0, gx < nx - 1
    low_ok, high_ok = gy > 0, gy < ny - 1
    low_f, high_f = jnp.where(low_ok, 1.0, 0.0), jnp.where(high_ok, 1.0, 0.0)
    edge_f = jnp.where(lane8 < 64, high_f, low_f)
    left_f, right_f = jnp.where(left_ok, 1.0, 0.0), jnp.where(right_ok, 1.0, 0.0)

    def rows(g):
        return pl.ds(8 * g, 8)

    def pack(e, parts, width, block, offset):
        per = 128 // block
        for v in range(-(-GROUPS // per)):
            value = jnp.zeros((8, 128), F32)
            for g in range(per * v, min(per * v + per, GROUPS)):
                for n, part in enumerate(parts[g]):
                    first = block * (g % per) + width * n
                    mine = (lane8 >= first) & (lane8 < first + width)
                    value = jnp.where(mine, roll(part, first + offset), value)
            packed[e, rows(v), :] = value

    inn[PLANES:] = jnp.zeros((PAD - PLANES, 16, 256), F32)
    gathered[PAD:] = jnp.zeros((MPAD - PAD, 512), F32)
    out_row, in_row = iota((48, 384), 0), iota((48, 384), 1) & 127
    same = (out_row & 7) == (in_row >> 4)
    off = (in_row & 15) - 4 * ((out_row >> 3) - 1)
    taps_x = jnp.where(same, tap(off, 4), 0.0).astype(BF16)
    taps_y[...] = tap(iota((256, 256), 0) - 2 * coarse_lane(iota((256, 256), 1)), 2).astype(BF16)

    loads[0].wait()
    loads[1].wait()

    def restrict_x(g, carry):
        at_g = pl.ds(pl.multiple_of(g * 8, 8), 8)
        block = (inn[at_g] * area[...][None]).reshape(128, 256)
        along[:, at_g, :] = dot(taps_x, pieces(block)).reshape(6, 8, 256)
        return carry

    lax.fori_loop(0, GROUPS, restrict_x, 0, unroll=3)
    part = dot(pieces(along[...].reshape(6 * PAD, 256)), taps_y[...])
    part = (part[: 6 * PAD] + part[6 * PAD : 12 * PAD] + part[12 * PAD :]) * (1.0 / 60.0)
    rest_low[...] = part[:, :128].reshape(6, PAD, 128)
    rest_high[...] = part[:, 128:].reshape(6, PAD, 128)

    pack(0, [[rest_high[r, rows(g), :] for r in range(6)] for g in range(GROUPS)], 2, 16, 1)

    pl.semaphore_wait(barrier, len(partners))

    def remote(source, target, send, recv, device):
        copy = pltpu.make_async_remote_copy(
            src_ref=source,
            dst_ref=target,
            send_sem=send,
            recv_sem=recv,
            device_id=device,
            device_id_type=MESH,
        )
        copy.start()
        return copy

    sent = []

    def inside(dx, dy):
        ok = None
        for here, step, size in ((gx, dx, nx), (gy, dy, ny)):
            if step:
                holds = here > 0 if step < 0 else here < size - 1
                ok = holds if ok is None else ok & holds
        return ok

    def send(moves):
        copies = []
        for dx, dy, source, target, send_sem, recv_sem in moves:
            copy = pltpu.make_async_remote_copy(
                src_ref=source,
                dst_ref=target,
                send_sem=send_sem,
                recv_sem=recv_sem,
                device_id=at(dx, dy),
                device_id_type=MESH,
            )
            pl.when(inside(dx, dy))(copy.start)
            copies.append((dx, dy, copy))
        sent.extend(copies)
        return copies

    def row_moves(e, to_left, at_right, to_right, at_left):
        return [
            (-1, 0, to_left, at_right, x_send.at[e, 0], x_recv.at[e, 1]),
            (1, 0, to_right, at_left, x_send.at[e, 1], x_recv.at[e, 0]),
        ]

    def side_moves(e):
        used = pl.ds(0, 16 if e == 0 else 24)
        return [
            (
                -sx,
                -sy,
                packed.at[e, used],
                packed_in.at[e, n, used],
                p_send.at[e, n],
                p_recv.at[e, n],
            )
            for n, (sx, sy) in sorted(enumerate(SIDES), key=lambda side: -abs(side[1][0]))
        ]

    def rim_rows(v):
        return row_moves(4 + v, ured.at[1, v], ured.at[5, v], ured.at[4, v], ured.at[0, v])

    def arrived(copies):
        for dx, dy, copy in copies:
            pl.when(inside(-dx, -dy))(copy.wait_recv)

    def sides(e, count, above):
        result = []
        for sx, ok in ((-1, left_ok), (0, None), (1, right_ok)):
            n = 2 * (sx + 1)
            there = jnp.where(above, high_f, low_f)
            if ok is not None:
                there = there * jnp.where(ok, 1.0, 0.0)
            result.append(
                [
                    jnp.where(
                        there > 0.5,
                        jnp.where(above, packed_in[e, n + 1, rows(v), :], packed_in[e, n, rows(v), :]),
                        0.0,
                    )
                    for v in range(count)
                ]
            )
        return result

    copies = send(
        side_moves(0) + row_moves(0, rest_low.at[0], rim_in.at[1], rest_low.at[5], rim_in.at[0])
    )

    for load in loads[2:]:
        load.wait()
    diagonal = iota((PAD, PLANES), 0) == iota((PAD, PLANES), 1)
    coef = jnp.sum(
        jnp.where(diagonal, jnp.broadcast_to(coef_ref[...], (PAD, PLANES)), 0.0),
        axis=1,
        keepdims=True,
    )
    coef_b[...] = jnp.broadcast_to(coef, (PAD, 128))
    coef_a[...] = jnp.broadcast_to(1.0 - 4.0 * coef, (PAD, 128))
    for i in range(4):
        sd[i, :PLANES] = sd_in[:, i, :]
        sd[i, PLANES:] = jnp.zeros((PAD - PLANES, 128), F32)
    cols = col_ref[...]
    cols_t = jnp.transpose(jnp.concatenate([cols.astype(F32), jnp.zeros((120, 128), F32)], axis=0))
    column = iota((512, 128), 0)
    for a in range(8):
        k = pl.ds(128 * a, 128)
        pick[:, k] = jnp.where(column == cols[a : a + 1], 1.0, 0.0).astype(BF16)
        of_slot = jnp.broadcast_to(cols_t[:, a : a + 1], (128, 512))
        place[k, :] = jnp.where(of_slot == iota((128, 512), 1).astype(F32), 1.0, 0.0).astype(BF16)
    obs_scale = prec_ref[...] * live_ref[...].astype(F32)
    scale = [
        jnp.concatenate([obs_scale[2 * n : 2 * n + 1], obs_scale[2 * n + 1 : 2 * n + 2]], axis=1)
        for n in range(4)
    ]

    arrived(copies)

    rim = sides(0, 2, (lane8 & 1) == 0)
    ends = (lane8 == 0) | (lane8 == 127)
    own = [[] for g in range(GROUPS)]
    for g in range(GROUPS):
        v, first = g // 8, 16 * (g % 8) + 1
        for i in range(4):
            value = rest_low[i + 1, rows(g), :]
            tails = roll(rim[1][v], -(first + 2 * (i + 1)))
            if i == 0:
                value = value + jnp.where(left_f > 0.5, rim_in[0, rows(g), :], 0.0)
                tails = tails + roll(rim[0][v], -(first + 10))
            if i == 3:
                value = value + jnp.where(right_f > 0.5, rim_in[1, rows(g), :], 0.0)
                tails = tails + roll(rim[2][v], -first)
            value = sd[i, rows(g), :] * (value + jnp.where(ends, tails, 0.0))
            field[0, 4 + i, rows(g), :] = value
            own[g].append(value)

    def pack_and_send(e, parts):
        pack(1 + e, parts, 8, 32, 4)
        own = field.at[e, pl.ds(4, 4)]
        after, before = field.at[e, pl.ds(8, 4)], field.at[e, pl.ds(0, 4)]
        return send(side_moves(1 + e) + row_moves(1 + e, own, after, own, before))

    def smooth(rows, first, coefs):
        result = []
        for n in range(1, len(rows) - 1):
            i = first + n
            a, b, a_high, b_high = coefs[0 if i < 0 else 1 if i < 4 else 2]
            (low, high), before, after = rows[n], rows[n - 1], rows[n + 1]
            of_low, of_high = beside(low, high, lane8)
            of_low = of_low + before[0] + after[0]
            of_high = of_high + before[1] + after[1]
            result.append((a * low + b * of_low, a_high * high + b_high * of_high))
        return result

    def smooth_step(e):
        tails = sides(1 + e, 3, (lane8 & 4) == 4)
        for g in range(GROUPS):
            at_g = rows(g)
            lines = []
            for r in range(12):
                low = field[e, r, at_g, :]
                if r < 4:
                    low = jnp.where(left_f > 0.5, low, 0.0)
                if r >= 8:
                    low = jnp.where(right_f > 0.5, low, 0.0)
                shift = 32 * (g % 4) + 8 * (r % 4) + 4
                lines.append((low, roll(tails[r // 4][g // 4], -shift)))
            a, b = coef_a[at_g, :], coef_b[at_g, :]
            coefs = [
                (a * f, b * f, a * f * edge_f, b * f * edge_f) for f in (left_f, F32(1.0), right_f)
            ]
            lines = smooth(smooth(lines, -4, coefs), -3, coefs)
            for i in range(4):
                base[e, i, at_g, :] = lines[2 + i][0]
            values = smooth(smooth(lines, -2, coefs), -1, coefs)
            for i, (low, _) in enumerate(values):
                pushed = sd[i, at_g, :] * low
                ured[1 + i, e, at_g, :] = pushed
                gathered[at_g, pl.ds(128 * i, 128)] = pushed

    def observe():
        left = pieces(gathered[...])
        seen = []
        for n in range(4):
            k = pl.ds(256 * n, 256)
            taken = dot(left, pick[:, k])
            taken = taken[:MPAD] + taken[MPAD : 2 * MPAD] + taken[2 * MPAD :]
            seen.append(jnp.sum(weight[:, k] * taken[:PLANES], axis=0, keepdims=True))
        return seen

    def scatter(seen):
        for n in range(4):
            k = pl.ds(256 * n, 256)
            back = weight[:, k] * (seen[n] * scale[n] * SCALE)
            back = jnp.concatenate([back, jnp.zeros((MPAD - PLANES, 256), F32)], axis=0)
            scaled[:, k] = pieces(back)

    def products(seen):
        parts = []
        for i, j in PAIRS:
            total = jnp.zeros((8, 128), F32)
            for g in range(GROUPS):
                for row in range(4):
                    total = total + base[i, row, rows(g), :] * base[j, row, rows(g), :]
            parts.append(jnp.sum(total, axis=0, keepdims=True))
        whole = []
        for (i, j), part in zip(PAIRS, parts):
            for n in range(4):
                square = scale[n] * seen[i][n] * seen[j][n]
                part = part + square[:, :128] + square[:, 128:]
            whole.append(part)
        whole += parts[:3]
        whole.append(jnp.zeros((16 - len(whole), 128), F32))
        total = jnp.sum(jnp.concatenate(whole, axis=0), axis=1, keepdims=True)
        mine = iota((16, 128), 0) == (iota((16, 128), 1) >> 3)
        msg_a[...] = jnp.sum(jnp.where(mine, total, 0.0), axis=0, keepdims=True)

    def put_back(e):
        own = [[] for g in range(GROUPS)]
        for h in range(2):
            value = dot(scaled[...], place[:, 256 * h : 256 * h + 256])
            value = value[:PAD] + value[MPAD : MPAD + PAD] + value[2 * MPAD : 2 * MPAD + PAD]
            for i in (2 * h, 2 * h + 1):
                row = sd[i] * value[:, 128 * (i % 2) : 128 * (i % 2) + 128]
                field[e, 4 + i] = row
                for g in range(GROUPS):
                    own[g].append(row[8 * g : 8 * g + 8])
        return own

    def reduce_start(msg, slots, send_sem, recv_sem, size, mine, partner):
        slots[mine] = msg[...]
        for o in sorted(range(1, size), key=lambda o: -min(o, size - o)):
            pltpu.make_async_remote_copy(
                src_ref=msg,
                dst_ref=slots.at[mine],
                send_sem=send_sem,
                recv_sem=recv_sem,
                device_id=partner(o),
                device_id_type=MESH,
            ).start()

    def all_of(slots, send_sem, recv_sem, size, partner):
        several = slots.at[pl.ds(0, size - 1)]
        return pltpu.make_async_remote_copy(
            src_ref=several,
            dst_ref=several,
            send_sem=send_sem,
            recv_sem=recv_sem,
            device_id=partner(1),
            device_id_type=MESH,
        )

    def total_of(slots, size):
        totals = [slots[o] for o in range(size)]
        while len(totals) > 1:
            totals = [sum(totals[n : n + 2]) for n in range(0, len(totals), 2)]
        return totals[0]

    def over_y(o):
        return at(0, o)

    def over_x(o):
        return at(o, 0)

    copies = pack_and_send(0, own)
    arrived(copies)
    smooth_step(0)
    seen = [observe()]
    scatter(seen[0])
    copies = pack_and_send(1, put_back(1))
    arrived(copies)

    rims = send(rim_rows(0))
    smooth_step(1)
    seen.append(observe())
    scatter(seen[1])
    copies = pack_and_send(2, put_back(2))
    arrived(copies)

    rims += send(rim_rows(1))
    smooth_step(2)
    edges = [
        [ured[1 + i, v, rows(g), :] for v in range(3) for i in range(4)] for g in range(GROUPS)
    ]
    pack(4, edges, 2, 32, 1)
    rims += send(side_moves(4) + rim_rows(2))
    seen.append(observe())
    products(seen)
    reduce_start(msg_a, slots_a, a_send, a_recv, ny, gy, over_y)

    for v in range(3):
        for i in range(4):
            ctl[v, i] = base[v, i]
    arrived(rims)
    tails = sides(4, 3, (lane8 & 1) == 1)
    out_row, in_col = iota((128, 48), 0), iota((128, 48), 1)
    off = (out_row & 15) - 4 * ((in_col >> 3) - 1)
    spread_x = jnp.where((in_col & 7) == (out_row >> 4), tap(off, 4), 0.0).astype(BF16)
    spread_x = jnp.concatenate([spread_x] * 3, axis=1)
    spread_y = tap(iota((256, 256), 1) - 2 * coarse_lane(iota((256, 256), 0)), 2).astype(BF16)
    sides_in = (lane8 == 0) | (lane8 == 127)

    def interpolate(v):
        for g in range(GROUPS):
            for r in range(6):
                value = ured[r, v, rows(g), :]
                if r == 0:
                    value = jnp.where(left_f > 0.5, value, 0.0)
                if r == 5:
                    value = jnp.where(right_f > 0.5, value, 0.0)
                sx = 0 if r == 0 else 2 if r == 5 else 1
                shift = 32 * (g % 4) + 8 * v + 2 * ((r - 1) % 4) + 1
                end = jnp.where(sides_in, roll(tails[sx][g // 4], -shift), 0.0)
                along[r, rows(g), :] = jnp.concatenate([value, end], axis=1)
        out = dot(pieces(along[...].reshape(6 * PAD, 256)), spread_y)
        out = (out[: 6 * PAD] + out[6 * PAD : 12 * PAD] + out[12 * PAD :]) * (1.0 / 60.0)
        out = out.reshape(6, PAD, 256)
        for g in range(GROUPS):
            part = dot(spread_x, pieces(out[:, 8 * g : 8 * g + 8, :].reshape(48, 256)))
            fine[v, rows(g)] = part.reshape(8, 16, 256)

    interpolate(0)
    sums_a = all_of(slots_a, a_send, a_recv, ny, over_y)
    sums_a.wait_recv()
    msg_b[...] = total_of(slots_a, ny)
    reduce_start(msg_b, slots_b, b_send, b_recv, nx, gx, over_x)
    interpolate(1)
    interpolate(2)
    sums_b = all_of(slots_b, b_send, b_recv, nx, over_x)
    sums_b.wait_recv()
    total = jnp.broadcast_to(total_of(slots_b, nx), (16, 128))
    mine = iota((16, 128), 0) * 8 == iota((16, 128), 1)
    total = jnp.sum(jnp.where(mine, total, 0.0), axis=1, keepdims=True)
    m00, m01, m02, m11, m12, m22, b0, b1, b2 = [
        jnp.broadcast_to(total[n : n + 1], (8, 128)) for n in range(9)
    ]

    def ratio(a, b):
        return jnp.where(b > 0.0, a / jnp.where(b > 0.0, b, 1.0), 0.0)

    l01, l02 = ratio(m01, m00), ratio(m02, m00)
    m11, m12, m22 = m11 - l01 * m01, m12 - l01 * m02, m22 - l02 * m02
    l12 = ratio(m12, m11)
    b1, b2 = b1 - l01 * b0, b2 - l02 * b0
    c2 = ratio(b2 - l12 * b1, m22 - l12 * m12)
    c1 = ratio(b1, m11) - l12 * c2
    steps[0] = ratio(b0, m00) - l01 * c1 - l02 * c2
    steps[1] = c1
    steps[2] = c2

    for dx, dy, copy in sent:
        pl.when(inside(dx, dy))(copy.wait_send)
    sums_a.wait_send()
    sums_b.wait_send()


def finish(parts, ctl, steps, fine_hbm, control, fine, sems):
    each = [jnp.concatenate([steps[v], steps[v]], axis=1) for v in range(3)]
    copies = []
    for g in range(GROUPS):
        count = min(8, PLANES - 8 * g)
        for p in range(8 * g, 8 * g + count):
            for h in range(2):
                at_h = pl.ds(8 * h, 8)
                fine[p, at_h, :] = sum(each[v] * parts[v, p, at_h, :] for v in range(3))
        planes = pl.ds(8 * g, count)
        copies.append(pltpu.make_async_copy(fine.at[planes], fine_hbm.at[planes], sems.at[g]))
        copies[-1].start()
    for i in range(4):
        value = sum(steps[v][:1] * ctl[v, i] for v in range(3))
        control[:, i, :] = value[:PLANES]
    for copy in copies:
        copy.wait()


def per_device(
    nx, ny, innovation, area, spread_sd, smooth_coef, obs_column, obs_weight, obs_precision, obs_live
):
    vmem, anywhere = pl.BlockSpec(memory_space=pltpu.VMEM), pl.BlockSpec(memory_space=pl.ANY)
    dma = pltpu.SemaphoreType.DMA
    fine, ctl, steps = pl.pallas_call(
        functools.partial(solve, nx, ny),
        out_shape=[
            jax.ShapeDtypeStruct((3, PAD, 16, 256), F32),
            jax.ShapeDtypeStruct((3, 4, PAD, 128), F32),
            jax.ShapeDtypeStruct((3, 8, 128), F32),
        ],
        in_specs=[pl.BlockSpec(memory_space=pltpu.HBM)] * 8,
        out_specs=[vmem, vmem, vmem],
        scratch_shapes=[
            pltpu.VMEM((PAD, 16, 256), F32),
            pltpu.VMEM((16, 256), F32),
            pltpu.VMEM((PLANES, 4, 128), F32),
            pltpu.VMEM((4, PAD, 128), F32),
            pltpu.VMEM((PLANES, 1024), F32),
            pltpu.VMEM((1, PLANES), F32),
            pltpu.VMEM((8, 128), jnp.int32),
            pltpu.VMEM((8, 128), F32),
            pltpu.VMEM((8, 128), jnp.int32),
            pltpu.VMEM((PAD, 128), F32),
            pltpu.VMEM((PAD, 128), F32),
            pltpu.VMEM((512, 1024), BF16),
            pltpu.VMEM((1024, 512), BF16),
            pltpu.VMEM((256, 256), BF16),
            pltpu.VMEM((6, PAD, 256), F32),
            pltpu.VMEM((6, PAD, 128), F32),
            pltpu.VMEM((6, PAD, 128), F32),
            pltpu.VMEM((2, PAD, 128), F32),
            pltpu.VMEM((3, 12, PAD, 128), F32),
            pltpu.VMEM((5, 24, 128), F32),
            pltpu.VMEM((5, 6, 24, 128), F32),
            pltpu.VMEM((3, 4, PAD, 128), F32),
            pltpu.VMEM((6, 3, PAD, 128), F32),
            pltpu.VMEM((MPAD, 512), F32),
            pltpu.VMEM((3 * MPAD, 1024), BF16),
            pltpu.VMEM((1, 128), F32),
            pltpu.VMEM((1, 128), F32),
            pltpu.VMEM((ny, 1, 128), F32),
            pltpu.VMEM((nx, 1, 128), F32),
            dma((8,)),
            dma((7, 2)),
            dma((7, 2)),
            dma((5, 6)),
            dma((5, 6)),
            dma,
            dma,
            dma,
            dma,
        ],
        compiler_params=pltpu.CompilerParams(
            collective_id=0, has_side_effects=True, vmem_limit_bytes=40 << 20
        ),
        name="solve",
    )(
        *(
            pltpu.with_memory_space_constraint(operand, pltpu.HBM)
            for operand in (
                innovation,
                area,
                spread_sd,
                smooth_coef.reshape(1, PLANES),
                obs_column.reshape(8, 128),
                obs_weight,
                obs_precision.reshape(8, 128),
                obs_live.reshape(8, 128),
            )
        )
    )
    return pl.pallas_call(
        finish,
        out_shape=[
            jax.ShapeDtypeStruct((PLANES, 16, 256), F32),
            jax.ShapeDtypeStruct((PLANES, 4, 128), F32),
        ],
        in_specs=[vmem, vmem, vmem],
        out_specs=[anywhere, vmem],
        scratch_shapes=[
            pltpu.VMEM((PAD, 16, 256), F32),
            dma((GROUPS,)),
        ],
        compiler_params=pltpu.CompilerParams(vmem_limit_bytes=24 << 20),
        name="finish",
    )(fine, ctl, steps)


def solution(mesh):
    nx, ny = mesh.shape["gx"], mesh.shape["gy"]
    return jax.shard_map(
        functools.partial(per_device, nx, ny),
        mesh=mesh,
        in_specs=(
            P(None, "gx", "gy"),
            P("gx", "gy"),
            P(None, "gx", "gy"),
            P(),
            P(("gx", "gy")),
            P(None, ("gx", "gy")),
            P(("gx", "gy")),
            P(("gx", "gy")),
        ),
        out_specs=(P(None, "gx", "gy"), P(None, "gx", "gy")),
        check_vma=False,
    )
```

```python
import functools

import jax
import jax.numpy as jnp
from jax import lax
from jax.experimental import pallas as pl
from jax.experimental.pallas import tpu as pltpu
from jax.sharding import PartitionSpec as P

F32 = jnp.float32
BF16 = jnp.bfloat16
MESH = pl.DeviceIdType.MESH
PLANES = 68
PAD = 72
MPAD = 80
GROUPS = PAD // 8
SCALE = 1.0 / 256.0
PAIRS = [(0, 0), (0, 1), (0, 2), (1, 1), (1, 2), (2, 2)]
SIDES = [(sx, sy) for sx in (-1, 0, 1) for sy in (-1, 1)]


def pieces(x):
    high = x.astype(BF16)
    rest = x - high.astype(F32)
    middle = rest.astype(BF16)
    low = (rest - middle.astype(F32)).astype(BF16)
    return jnp.concatenate([high, middle, low], axis=0)


def dot(a, b):
    return jnp.dot(a, b, preferred_element_type=F32)


def iota(shape, dim):
    return lax.broadcasted_iota(jnp.int32, shape, dim)


def tap(offset, ratio):
    inner = (offset >= 0) & (offset < ratio)
    ends = (offset == -1) | (offset == ratio)
    return jnp.where(inner, 2.0, jnp.where(ends, 1.0, 0.0))


def coarse_lane(lane):
    return jnp.where(lane == 255, -1, lane)


def roll(x, shift):
    return pltpu.roll(x, shift % 128, x.ndim - 1)


def beside(low, high, lane):
    low_up, low_down = roll(low, 1), roll(low, 127)
    high_up, high_down = roll(high, 1), roll(high, 127)
    first, last = lane == 0, lane == 127
    of_low = jnp.where(first, high_up, low_up) + jnp.where(last, high_down, low_down)
    of_high = jnp.where(first, low_up, high_up) + jnp.where(last, low_down, high_down)
    return of_low, of_high


def solve(
    nx,
    ny,
    inn_hbm,
    area_hbm,
    sd_hbm,
    coef_hbm,
    col_hbm,
    weight_hbm,
    prec_hbm,
    live_hbm,
    fine,
    ctl,
    steps,
    inn,
    area,
    sd_in,
    sd,
    weight,
    coef_ref,
    col_ref,
    prec_ref,
    live_ref,
    coef_a,
    coef_b,
    pick,
    place,
    taps_y,
    along,
    rest_low,
    rest_high,
    rim_in,
    field,
    packed,
    packed_in,
    base,
    base_high,
    high_in,
    once_low,
    once_high,
    ured,
    gathered,
    scaled,
    msg_a,
    msg_b,
    slots_a,
    slots_b,
    in_sems,
    x_send,
    x_recv,
    p_send,
    p_recv,
    a_send,
    a_recv,
    b_send,
    b_recv,
):
    gx, gy = lax.axis_index("gx"), lax.axis_index("gy")

    def shifted(here, step, size):
        if step == 0:
            return here
        if size & (size - 1) == 0:
            return (here + (step + size)) & (size - 1)
        return lax.rem(here + (step + size), size)

    def at(dx, dy):
        return (shifted(gx, dx, nx), shifted(gy, dy, ny))

    loads = [
        pltpu.make_async_copy(inn_hbm, inn.at[pl.ds(0, PLANES)], in_sems.at[0]),
        pltpu.make_async_copy(area_hbm, area, in_sems.at[1]),
        pltpu.make_async_copy(sd_hbm, sd_in, in_sems.at[2]),
        pltpu.make_async_copy(weight_hbm, weight, in_sems.at[3]),
        pltpu.make_async_copy(coef_hbm, coef_ref, in_sems.at[4]),
        pltpu.make_async_copy(col_hbm, col_ref, in_sems.at[5]),
        pltpu.make_async_copy(prec_hbm, prec_ref, in_sems.at[6]),
        pltpu.make_async_copy(live_hbm, live_ref, in_sems.at[7]),
    ]
    for load in loads:
        load.start()

    barrier = pltpu.get_barrier_semaphore()
    partners = [at(0, o) for o in range(1, ny)] + [at(o, 0) for o in range(1, nx)]
    partners += [at(dx, dy) for dx in (-1, 1) for dy in (-1, 1)]
    for partner in partners:
        pl.semaphore_signal(barrier, inc=1, device_id=partner, device_id_type=MESH)

    lane8 = iota((8, 128), 1)
    left_ok, right_ok = gx > 0, gx < nx - 1
    low_ok, high_ok = gy > 0, gy < ny - 1
    low_f, high_f = jnp.where(low_ok, 1.0, 0.0), jnp.where(high_ok, 1.0, 0.0)
    edge_f = jnp.where(lane8 < 64, high_f, low_f)
    left_f, right_f = jnp.where(left_ok, 1.0, 0.0), jnp.where(right_ok, 1.0, 0.0)

    def rows(g):
        return pl.ds(8 * g, 8)

    def pack(e, parts, width, block, offset):
        per = 128 // block
        for v in range(-(-GROUPS // per)):
            value = jnp.zeros((8, 128), F32)
            for g in range(per * v, min(per * v + per, GROUPS)):
                for n, part in enumerate(parts[g]):
                    first = block * (g % per) + width * n
                    mine = (lane8 >= first) & (lane8 < first + width)
                    value = jnp.where(mine, roll(part, first + offset), value)
            packed[e, rows(v), :] = value

    inn[PLANES:] = jnp.zeros((PAD - PLANES, 16, 256), F32)
    gathered[PAD:] = jnp.zeros((MPAD - PAD, 512), F32)
    out_row, in_row = iota((48, 384), 0), iota((48, 384), 1) & 127
    same = (out_row & 7) == (in_row >> 4)
    off = (in_row & 15) - 4 * ((out_row >> 3) - 1)
    taps_x = jnp.where(same, tap(off, 4), 0.0).astype(BF16)
    taps_y[...] = tap(iota((256, 256), 0) - 2 * coarse_lane(iota((256, 256), 1)), 2).astype(BF16)

    loads[0].wait()
    loads[1].wait()

    def restrict_x(g, carry):
        at_g = pl.ds(pl.multiple_of(g * 8, 8), 8)
        block = (inn[at_g] * area[...][None]).reshape(128, 256)
        along[:, at_g, :] = dot(taps_x, pieces(block)).reshape(6, 8, 256)
        return carry

    lax.fori_loop(0, GROUPS, restrict_x, 0, unroll=3)
    part = dot(pieces(along[...].reshape(6 * PAD, 256)), taps_y[...])
    part = (part[: 6 * PAD] + part[6 * PAD : 12 * PAD] + part[12 * PAD :]) * (1.0 / 60.0)
    rest_low[...] = part[:, :128].reshape(6, PAD, 128)
    rest_high[...] = part[:, 128:].reshape(6, PAD, 128)

    pack(0, [[rest_high[r, rows(g), :] for r in range(6)] for g in range(GROUPS)], 2, 16, 1)

    pl.semaphore_wait(barrier, len(partners))

    def remote(source, target, send, recv, device):
        copy = pltpu.make_async_remote_copy(
            src_ref=source,
            dst_ref=target,
            send_sem=send,
            recv_sem=recv,
            device_id=device,
            device_id_type=MESH,
        )
        copy.start()
        return copy

    sent = []

    def inside(dx, dy):
        ok = None
        for here, step, size in ((gx, dx, nx), (gy, dy, ny)):
            if step:
                holds = here > 0 if step < 0 else here < size - 1
                ok = holds if ok is None else ok & holds
        return ok

    def send(moves):
        copies = []
        for dx, dy, source, target, send_sem, recv_sem in moves:
            copy = pltpu.make_async_remote_copy(
                src_ref=source,
                dst_ref=target,
                send_sem=send_sem,
                recv_sem=recv_sem,
                device_id=at(dx, dy),
                device_id_type=MESH,
            )
            pl.when(inside(dx, dy))(copy.start)
            copies.append((dx, dy, copy))
        sent.extend(copies)
        return copies

    def row_moves(e, to_left, at_right, to_right, at_left):
        return [
            (-1, 0, to_left, at_right, x_send.at[e, 0], x_recv.at[e, 1]),
            (1, 0, to_right, at_left, x_send.at[e, 1], x_recv.at[e, 0]),
        ]

    def side_moves(e):
        used = pl.ds(0, 16 if e == 0 else 24)
        return [
            (
                -sx,
                -sy,
                packed.at[e, used],
                packed_in.at[e, n, used],
                p_send.at[e, n],
                p_recv.at[e, n],
            )
            for n, (sx, sy) in sorted(enumerate(SIDES), key=lambda side: -abs(side[1][0]))
        ]

    def rim_rows(v):
        return row_moves(4 + v, ured.at[1, v], ured.at[5, v], ured.at[4, v], ured.at[0, v])

    def arrived(copies):
        for dx, dy, copy in copies:
            pl.when(inside(-dx, -dy))(copy.wait_recv)

    def sides(e, count, above):
        result = []
        for sx, ok in ((-1, left_ok), (0, None), (1, right_ok)):
            n = 2 * (sx + 1)
            there = jnp.where(above, high_f, low_f)
            if ok is not None:
                there = there * jnp.where(ok, 1.0, 0.0)
            result.append(
                [
                    jnp.where(
                        there > 0.5,
                        jnp.where(above, packed_in[e, n + 1, rows(v), :], packed_in[e, n, rows(v), :]),
                        0.0,
                    )
                    for v in range(count)
                ]
            )
        return result

    copies = send(
        side_moves(0)[:4]
        + row_moves(0, rest_low.at[0], rim_in.at[1], rest_low.at[5], rim_in.at[0])
        + side_moves(0)[4:]
    )

    for load in loads[2:]:
        load.wait()
    diagonal = iota((PAD, PLANES), 0) == iota((PAD, PLANES), 1)
    coef = jnp.sum(
        jnp.where(diagonal, jnp.broadcast_to(coef_ref[...], (PAD, PLANES)), 0.0),
        axis=1,
        keepdims=True,
    )
    coef_b[...] = jnp.broadcast_to(coef, (PAD, 128))
    coef_a[...] = jnp.broadcast_to(1.0 - 4.0 * coef, (PAD, 128))
    for i in range(4):
        sd[i, :PLANES] = sd_in[:, i, :]
        sd[i, PLANES:] = jnp.zeros((PAD - PLANES, 128), F32)
    cols = col_ref[...]
    cols_t = jnp.transpose(jnp.concatenate([cols.astype(F32), jnp.zeros((120, 128), F32)], axis=0))
    column = iota((512, 128), 0)
    for a in range(8):
        k = pl.ds(128 * a, 128)
        pick[:, k] = jnp.where(column == cols[a : a + 1], 1.0, 0.0).astype(BF16)
        of_slot = jnp.broadcast_to(cols_t[:, a : a + 1], (128, 512))
        place[k, :] = jnp.where(of_slot == iota((128, 512), 1).astype(F32), 1.0, 0.0).astype(BF16)
    obs_scale = prec_ref[...] * live_ref[...].astype(F32)
    scale = [
        jnp.concatenate([obs_scale[2 * n : 2 * n + 1], obs_scale[2 * n + 1 : 2 * n + 2]], axis=1)
        for n in range(4)
    ]

    arrived(copies)

    rim = sides(0, 2, (lane8 & 1) == 0)
    ends = (lane8 == 0) | (lane8 == 127)
    own = [[] for g in range(GROUPS)]
    for g in range(GROUPS):
        v, first = g // 8, 16 * (g % 8) + 1
        for i in range(4):
            value = rest_low[i + 1, rows(g), :]
            tails = roll(rim[1][v], -(first + 2 * (i + 1)))
            if i == 0:
                value = value + jnp.where(left_f > 0.5, rim_in[0, rows(g), :], 0.0)
                tails = tails + roll(rim[0][v], -(first + 10))
            if i == 3:
                value = value + jnp.where(right_f > 0.5, rim_in[1, rows(g), :], 0.0)
                tails = tails + roll(rim[2][v], -first)
            value = sd[i, rows(g), :] * (value + jnp.where(ends, tails, 0.0))
            field[0, 4 + i, rows(g), :] = value
            own[g].append(value)

    def pack_and_send(e, parts):
        pack(1 + e, parts, 8, 32, 4)
        def part(r):
            return field.at[e, pl.ds(r, 2)]

        near = row_moves(1 + e, part(4), part(8), part(6), part(2))
        far = row_moves(7 + e, part(6), part(10), part(4), part(0))
        side = side_moves(1 + e)
        copies = send(side[:4] + near + side[4:] + far)
        return copies[:-2], copies[-2:]

    def smooth(rows, first, coefs):
        result = []
        for n in range(1, len(rows) - 1):
            i = first + n
            a, b, a_high, b_high = coefs[0 if i < 0 else 1 if i < 4 else 2]
            (low, high), before, after = rows[n], rows[n - 1], rows[n + 1]
            of_low, of_high = beside(low, high, lane8)
            of_low = of_low + before[0] + after[0]
            of_high = of_high + before[1] + after[1]
            result.append((a * low + b * of_low, a_high * high + b_high * of_high))
        return result

    def coefficients(g):
        a, b = coef_a[rows(g), :], coef_b[rows(g), :]
        return [(a * f, b * f, a * f * edge_f, b * f * edge_f) for f in (left_f, F32(1.0), right_f)]

    def line(e, g, r):
        low = field[e, r, rows(g), :]
        if r < 4:
            low = jnp.where(left_f > 0.5, low, 0.0)
        if r >= 8:
            low = jnp.where(right_f > 0.5, low, 0.0)
        return low

    def side(tails, g, r):
        return roll(tails[r // 4][g // 4], -(32 * (g % 4) + 8 * (r % 4) + 4))

    def smooth_near(e):
        tails = sides(1 + e, 3, (lane8 & 4) == 4)
        for g in range(GROUPS):
            at_g, coefs = rows(g), coefficients(g)
            lines = [(line(e, g, r), side(tails, g, r)) for r in range(2, 10)]
            for n, k in enumerate((0, 1, 6, 7)):
                high_in[n, at_g, :] = lines[k][1]
            once = smooth(lines, -2, coefs)
            for n, k in enumerate((0, 1, 4, 5)):
                once_low[n, at_g, :], once_high[n, at_g, :] = once[k]
            for i, (low, high) in enumerate(smooth(once, -1, coefs)):
                base[e, i, at_g, :] = low
                base_high[i, at_g, :] = high

    def smooth_far(e):
        tails = sides(1 + e, 3, (lane8 & 4) == 4)
        for g in range(GROUPS):
            at_g, coefs = rows(g), coefficients(g)
            above = [(line(e, g, r), side(tails, g, r)) for r in (0, 1)]
            above += [(line(e, g, 2 + n), high_in[n, at_g, :]) for n in (0, 1)]
            below = [(line(e, g, 6 + n), high_in[n, at_g, :]) for n in (2, 3)]
            below += [(line(e, g, r), side(tails, g, r)) for r in (10, 11)]
            once = [(once_low[n, at_g, :], once_high[n, at_g, :]) for n in range(4)]
            above = smooth(smooth(above, -4, coefs) + once[:2], -3, coefs)
            below = smooth(once[2:] + smooth(below, 4, coefs), 3, coefs)
            own = [(base[e, i, at_g, :], base_high[i, at_g, :]) for i in range(4)]
            values = smooth(smooth(above + own + below, -2, coefs), -1, coefs)
            for i, (low, _) in enumerate(values):
                pushed = sd[i, at_g, :] * low
                ured[1 + i, e, at_g, :] = pushed
                gathered[at_g, pl.ds(128 * i, 128)] = pushed

    def observe():
        left = pieces(gathered[...])
        seen = []
        for n in range(4):
            k = pl.ds(256 * n, 256)
            taken = dot(left, pick[:, k])
            taken = taken[:MPAD] + taken[MPAD : 2 * MPAD] + taken[2 * MPAD :]
            seen.append(jnp.sum(weight[:, k] * taken[:PLANES], axis=0, keepdims=True))
        return seen

    def scatter(seen):
        for n in range(4):
            k = pl.ds(256 * n, 256)
            back = weight[:, k] * (seen[n] * scale[n] * SCALE)
            back = jnp.concatenate([back, jnp.zeros((MPAD - PLANES, 256), F32)], axis=0)
            scaled[:, k] = pieces(back)

    def products(seen):
        parts = []
        for i, j in PAIRS:
            total = jnp.zeros((8, 128), F32)
            for g in range(GROUPS):
                for row in range(4):
                    total = total + base[i, row, rows(g), :] * base[j, row, rows(g), :]
            parts.append(jnp.sum(total, axis=0, keepdims=True))
        whole = []
        for (i, j), part in zip(PAIRS, parts):
            for n in range(4):
                square = scale[n] * seen[i][n] * seen[j][n]
                part = part + square[:, :128] + square[:, 128:]
            whole.append(part)
        whole += parts[:3]
        whole.append(jnp.zeros((16 - len(whole), 128), F32))
        total = jnp.sum(jnp.concatenate(whole, axis=0), axis=1, keepdims=True)
        mine = iota((16, 128), 0) == (iota((16, 128), 1) >> 3)
        msg_a[...] = jnp.sum(jnp.where(mine, total, 0.0), axis=0, keepdims=True)

    def put_back(e):
        own = [[] for g in range(GROUPS)]
        for h in range(2):
            value = dot(scaled[...], place[:, 256 * h : 256 * h + 256])
            value = value[:PAD] + value[MPAD : MPAD + PAD] + value[2 * MPAD : 2 * MPAD + PAD]
            for i in (2 * h, 2 * h + 1):
                row = sd[i] * value[:, 128 * (i % 2) : 128 * (i % 2) + 128]
                field[e, 4 + i] = row
                for g in range(GROUPS):
                    own[g].append(row[8 * g : 8 * g + 8])
        return own

    def reduce_start(msg, slots, send_sem, recv_sem, size, mine, partner):
        slots[mine] = msg[...]
        for o in sorted(range(1, size), key=lambda o: -min(o, size - o)):
            pltpu.make_async_remote_copy(
                src_ref=msg,
                dst_ref=slots.at[mine],
                send_sem=send_sem,
                recv_sem=recv_sem,
                device_id=partner(o),
                device_id_type=MESH,
            ).start()

    def all_of(slots, send_sem, recv_sem, size, partner):
        several = slots.at[pl.ds(0, size - 1)]
        return pltpu.make_async_remote_copy(
            src_ref=several,
            dst_ref=several,
            send_sem=send_sem,
            recv_sem=recv_sem,
            device_id=partner(1),
            device_id_type=MESH,
        )

    def total_of(slots, size):
        totals = [slots[o] for o in range(size)]
        while len(totals) > 1:
            totals = [sum(totals[n : n + 2]) for n in range(0, len(totals), 2)]
        return totals[0]

    def over_y(o):
        return at(0, o)

    def over_x(o):
        return at(o, 0)

    near, far = pack_and_send(0, own)
    arrived(near)
    smooth_near(0)
    arrived(far)
    smooth_far(0)
    seen = [observe()]
    scatter(seen[0])
    near, far = pack_and_send(1, put_back(1))
    arrived(near)
    smooth_near(1)
    arrived(far)
    rims = send(rim_rows(0))
    smooth_far(1)
    seen.append(observe())
    scatter(seen[1])
    near, far = pack_and_send(2, put_back(2))
    arrived(near)
    smooth_near(2)
    arrived(far)
    rims += send(rim_rows(1))
    smooth_far(2)
    edges = [
        [ured[1 + i, v, rows(g), :] for v in range(3) for i in range(4)] for g in range(GROUPS)
    ]
    pack(4, edges, 2, 32, 1)
    rims += send(side_moves(4) + rim_rows(2))
    seen.append(observe())
    products(seen)
    reduce_start(msg_a, slots_a, a_send, a_recv, ny, gy, over_y)

    for v in range(3):
        for i in range(4):
            ctl[v, i] = base[v, i]
    sums_a = all_of(slots_a, a_send, a_recv, ny, over_y)
    sums_a.wait_recv()
    msg_b[...] = total_of(slots_a, ny)
    reduce_start(msg_b, slots_b, b_send, b_recv, nx, gx, over_x)
    arrived(rims)
    tails = sides(4, 3, (lane8 & 1) == 1)
    out_row, in_col = iota((128, 48), 0), iota((128, 48), 1)
    off = (out_row & 15) - 4 * ((in_col >> 3) - 1)
    spread_x = jnp.where((in_col & 7) == (out_row >> 4), tap(off, 4), 0.0).astype(BF16)
    spread_x = jnp.concatenate([spread_x] * 3, axis=1)
    spread_y = tap(iota((256, 256), 1) - 2 * coarse_lane(iota((256, 256), 0)), 2).astype(BF16)
    sides_in = (lane8 == 0) | (lane8 == 127)

    def interpolate(v):
        for g in range(GROUPS):
            for r in range(6):
                value = ured[r, v, rows(g), :]
                if r == 0:
                    value = jnp.where(left_f > 0.5, value, 0.0)
                if r == 5:
                    value = jnp.where(right_f > 0.5, value, 0.0)
                sx = 0 if r == 0 else 2 if r == 5 else 1
                shift = 32 * (g % 4) + 8 * v + 2 * ((r - 1) % 4) + 1
                end = jnp.where(sides_in, roll(tails[sx][g // 4], -shift), 0.0)
                along[r, rows(g), :] = jnp.concatenate([value, end], axis=1)
        out = dot(pieces(along[...].reshape(6 * PAD, 256)), spread_y)
        out = (out[: 6 * PAD] + out[6 * PAD : 12 * PAD] + out[12 * PAD :]) * (1.0 / 60.0)
        out = out.reshape(6, PAD, 256)
        for g in range(GROUPS):
            part = dot(spread_x, pieces(out[:, 8 * g : 8 * g + 8, :].reshape(48, 256)))
            fine[v, rows(g)] = part.reshape(8, 16, 256)

    interpolate(0)
    interpolate(1)
    interpolate(2)
    sums_b = all_of(slots_b, b_send, b_recv, nx, over_x)
    sums_b.wait_recv()
    total = jnp.broadcast_to(total_of(slots_b, nx), (16, 128))
    mine = iota((16, 128), 0) * 8 == iota((16, 128), 1)
    total = jnp.sum(jnp.where(mine, total, 0.0), axis=1, keepdims=True)
    m00, m01, m02, m11, m12, m22, b0, b1, b2 = [
        jnp.broadcast_to(total[n : n + 1], (8, 128)) for n in range(9)
    ]

    def ratio(a, b):
        return jnp.where(b > 0.0, a / jnp.where(b > 0.0, b, 1.0), 0.0)

    l01, l02 = ratio(m01, m00), ratio(m02, m00)
    m11, m12, m22 = m11 - l01 * m01, m12 - l01 * m02, m22 - l02 * m02
    l12 = ratio(m12, m11)
    b1, b2 = b1 - l01 * b0, b2 - l02 * b0
    c2 = ratio(b2 - l12 * b1, m22 - l12 * m12)
    c1 = ratio(b1, m11) - l12 * c2
    steps[0] = ratio(b0, m00) - l01 * c1 - l02 * c2
    steps[1] = c1
    steps[2] = c2

    for dx, dy, copy in sent:
        pl.when(inside(dx, dy))(copy.wait_send)
    sums_a.wait_send()
    sums_b.wait_send()


def finish(parts, ctl, steps, fine_hbm, control, fine, sems):
    each = [jnp.concatenate([steps[v], steps[v]], axis=1) for v in range(3)]
    copies = []
    for g in range(GROUPS):
        count = min(8, PLANES - 8 * g)
        for p in range(8 * g, 8 * g + count):
            for h in range(2):
                at_h = pl.ds(8 * h, 8)
                fine[p, at_h, :] = sum(each[v] * parts[v, p, at_h, :] for v in range(3))
        planes = pl.ds(8 * g, count)
        copies.append(pltpu.make_async_copy(fine.at[planes], fine_hbm.at[planes], sems.at[g]))
        copies[-1].start()
    for i in range(4):
        value = sum(steps[v][:1] * ctl[v, i] for v in range(3))
        control[:, i, :] = value[:PLANES]
    for copy in copies:
        copy.wait()


def per_device(
    nx, ny, innovation, area, spread_sd, smooth_coef, obs_column, obs_weight, obs_precision, obs_live
):
    vmem, anywhere = pl.BlockSpec(memory_space=pltpu.VMEM), pl.BlockSpec(memory_space=pl.ANY)
    dma = pltpu.SemaphoreType.DMA
    fine, ctl, steps = pl.pallas_call(
        functools.partial(solve, nx, ny),
        out_shape=[
            jax.ShapeDtypeStruct((3, PAD, 16, 256), F32),
            jax.ShapeDtypeStruct((3, 4, PAD, 128), F32),
            jax.ShapeDtypeStruct((3, 8, 128), F32),
        ],
        in_specs=[pl.BlockSpec(memory_space=pltpu.HBM)] * 8,
        out_specs=[vmem, vmem, vmem],
        scratch_shapes=[
            pltpu.VMEM((PAD, 16, 256), F32),
            pltpu.VMEM((16, 256), F32),
            pltpu.VMEM((PLANES, 4, 128), F32),
            pltpu.VMEM((4, PAD, 128), F32),
            pltpu.VMEM((PLANES, 1024), F32),
            pltpu.VMEM((1, PLANES), F32),
            pltpu.VMEM((8, 128), jnp.int32),
            pltpu.VMEM((8, 128), F32),
            pltpu.VMEM((8, 128), jnp.int32),
            pltpu.VMEM((PAD, 128), F32),
            pltpu.VMEM((PAD, 128), F32),
            pltpu.VMEM((512, 1024), BF16),
            pltpu.VMEM((1024, 512), BF16),
            pltpu.VMEM((256, 256), BF16),
            pltpu.VMEM((6, PAD, 256), F32),
            pltpu.VMEM((6, PAD, 128), F32),
            pltpu.VMEM((6, PAD, 128), F32),
            pltpu.VMEM((2, PAD, 128), F32),
            pltpu.VMEM((3, 12, PAD, 128), F32),
            pltpu.VMEM((5, 24, 128), F32),
            pltpu.VMEM((5, 6, 24, 128), F32),
            pltpu.VMEM((3, 4, PAD, 128), F32),
            pltpu.VMEM((4, PAD, 128), F32),
            pltpu.VMEM((4, PAD, 128), F32),
            pltpu.VMEM((4, PAD, 128), F32),
            pltpu.VMEM((4, PAD, 128), F32),
            pltpu.VMEM((6, 3, PAD, 128), F32),
            pltpu.VMEM((MPAD, 512), F32),
            pltpu.VMEM((3 * MPAD, 1024), BF16),
            pltpu.VMEM((1, 128), F32),
            pltpu.VMEM((1, 128), F32),
            pltpu.VMEM((ny, 1, 128), F32),
            pltpu.VMEM((nx, 1, 128), F32),
            dma((8,)),
            dma((10, 2)),
            dma((10, 2)),
            dma((5, 6)),
            dma((5, 6)),
            dma,
            dma,
            dma,
            dma,
        ],
        compiler_params=pltpu.CompilerParams(
            collective_id=0, has_side_effects=True, vmem_limit_bytes=40 << 20
        ),
        name="solve",
    )(
        *(
            pltpu.with_memory_space_constraint(operand, pltpu.HBM)
            for operand in (
                innovation,
                area,
                spread_sd,
                smooth_coef.reshape(1, PLANES),
                obs_column.reshape(8, 128),
                obs_weight,
                obs_precision.reshape(8, 128),
                obs_live.reshape(8, 128),
            )
        )
    )
    return pl.pallas_call(
        finish,
        out_shape=[
            jax.ShapeDtypeStruct((PLANES, 16, 256), F32),
            jax.ShapeDtypeStruct((PLANES, 4, 128), F32),
        ],
        in_specs=[vmem, vmem, vmem],
        out_specs=[anywhere, vmem],
        scratch_shapes=[
            pltpu.VMEM((PAD, 16, 256), F32),
            dma((GROUPS,)),
        ],
        compiler_params=pltpu.CompilerParams(vmem_limit_bytes=24 << 20),
        name="finish",
    )(fine, ctl, steps)


def solution(mesh):
    nx, ny = mesh.shape["gx"], mesh.shape["gy"]
    return jax.shard_map(
        functools.partial(per_device, nx, ny),
        mesh=mesh,
        in_specs=(
            P(None, "gx", "gy"),
            P("gx", "gy"),
            P(None, "gx", "gy"),
            P(),
            P(("gx", "gy")),
            P(None, ("gx", "gy")),
            P(("gx", "gy")),
            P(("gx", "gy")),
        ),
        out_specs=(P(None, "gx", "gy"), P(None, "gx", "gy")),
        check_vma=False,
    )
```

```python
import functools

import jax
import jax.numpy as jnp
from jax import lax
from jax.experimental import pallas as pl
from jax.experimental.pallas import tpu as pltpu
from jax.sharding import PartitionSpec as P

F32 = jnp.float32
BF16 = jnp.bfloat16
MESH = pl.DeviceIdType.MESH
PLANES = 68
PAD = 72
MPAD = 80
GROUPS = PAD // 8
SCALE = 1.0 / 256.0
PAIRS = [(0, 0), (0, 1), (0, 2), (1, 1), (1, 2), (2, 2)]
SIDES = [(sx, sy) for sx in (-1, 0, 1) for sy in (-1, 1)]


def pieces(x):
    high = x.astype(BF16)
    rest = x - high.astype(F32)
    middle = rest.astype(BF16)
    low = (rest - middle.astype(F32)).astype(BF16)
    return jnp.concatenate([high, middle, low], axis=0)


def dot(a, b):
    return jnp.dot(a, b, preferred_element_type=F32)


def iota(shape, dim):
    return lax.broadcasted_iota(jnp.int32, shape, dim)


def tap(offset, ratio):
    inner = (offset >= 0) & (offset < ratio)
    ends = (offset == -1) | (offset == ratio)
    return jnp.where(inner, 2.0, jnp.where(ends, 1.0, 0.0))


def coarse_lane(lane):
    return jnp.where(lane == 255, -1, lane)


def roll(x, shift):
    return pltpu.roll(x, shift % 128, x.ndim - 1)


def beside(low, high, lane):
    low_up, low_down = roll(low, 1), roll(low, 127)
    high_up, high_down = roll(high, 1), roll(high, 127)
    first, last = lane == 0, lane == 127
    of_low = jnp.where(first, high_up, low_up) + jnp.where(last, high_down, low_down)
    of_high = jnp.where(first, low_up, high_up) + jnp.where(last, low_down, high_down)
    return of_low, of_high


def solve(
    nx,
    ny,
    inn_hbm,
    area_hbm,
    sd_hbm,
    coef_hbm,
    col_hbm,
    weight_hbm,
    prec_hbm,
    live_hbm,
    fine,
    ctl,
    steps,
    inn,
    area,
    sd_in,
    sd,
    weight,
    coef_ref,
    col_ref,
    prec_ref,
    live_ref,
    coef_a,
    coef_b,
    pick,
    place,
    taps_y,
    along,
    rest_low,
    rest_high,
    rim_in,
    field,
    packed,
    packed_in,
    base,
    base_high,
    high_in,
    once_low,
    once_high,
    ured,
    gathered,
    scaled,
    msg_a,
    msg_b,
    slots_a,
    slots_b,
    in_sems,
    x_send,
    x_recv,
    p_send,
    p_recv,
    a_send,
    a_recv,
    b_send,
    b_recv,
):
    gx, gy = lax.axis_index("gx"), lax.axis_index("gy")

    def shifted(here, step, size):
        if step == 0:
            return here
        if size & (size - 1) == 0:
            return (here + (step + size)) & (size - 1)
        return lax.rem(here + (step + size), size)

    def at(dx, dy):
        return (shifted(gx, dx, nx), shifted(gy, dy, ny))

    loads = [
        pltpu.make_async_copy(inn_hbm, inn.at[pl.ds(0, PLANES)], in_sems.at[0]),
        pltpu.make_async_copy(area_hbm, area, in_sems.at[1]),
        pltpu.make_async_copy(sd_hbm, sd_in, in_sems.at[2]),
        pltpu.make_async_copy(weight_hbm, weight, in_sems.at[3]),
        pltpu.make_async_copy(coef_hbm, coef_ref, in_sems.at[4]),
        pltpu.make_async_copy(col_hbm, col_ref, in_sems.at[5]),
        pltpu.make_async_copy(prec_hbm, prec_ref, in_sems.at[6]),
        pltpu.make_async_copy(live_hbm, live_ref, in_sems.at[7]),
    ]
    for load in loads:
        load.start()

    barrier = pltpu.get_barrier_semaphore()
    partners = [at(0, o) for o in range(1, ny)] + [at(o, 0) for o in range(1, nx)]
    partners += [at(dx, dy) for dx in (-1, 1) for dy in (-1, 1)]
    for partner in partners:
        pl.semaphore_signal(barrier, inc=1, device_id=partner, device_id_type=MESH)

    lane8 = iota((8, 128), 1)
    left_ok, right_ok = gx > 0, gx < nx - 1
    low_ok, high_ok = gy > 0, gy < ny - 1
    low_f, high_f = jnp.where(low_ok, 1.0, 0.0), jnp.where(high_ok, 1.0, 0.0)
    edge_f = jnp.where(lane8 < 64, high_f, low_f)
    left_f, right_f = jnp.where(left_ok, 1.0, 0.0), jnp.where(right_ok, 1.0, 0.0)

    def rows(g):
        return pl.ds(8 * g, 8)

    def pack(e, parts, width, block, offset):
        per = 128 // block
        for v in range(-(-GROUPS // per)):
            value = jnp.zeros((8, 128), F32)
            for g in range(per * v, min(per * v + per, GROUPS)):
                for n, part in enumerate(parts[g]):
                    first = block * (g % per) + width * n
                    mine = (lane8 >= first) & (lane8 < first + width)
                    value = jnp.where(mine, roll(part, first + offset), value)
            packed[e, rows(v), :] = value

    inn[PLANES:] = jnp.zeros((PAD - PLANES, 16, 256), F32)
    gathered[PAD:] = jnp.zeros((MPAD - PAD, 512), F32)
    out_row, in_row = iota((48, 384), 0), iota((48, 384), 1) & 127
    same = (out_row & 7) == (in_row >> 4)
    off = (in_row & 15) - 4 * ((out_row >> 3) - 1)
    taps_x = jnp.where(same, tap(off, 4), 0.0).astype(BF16)
    taps_y[...] = tap(iota((256, 256), 0) - 2 * coarse_lane(iota((256, 256), 1)), 2).astype(BF16)

    loads[0].wait()
    loads[1].wait()

    def restrict_x(g, carry):
        at_g = pl.ds(pl.multiple_of(g * 8, 8), 8)
        block = (inn[at_g] * area[...][None]).reshape(128, 256)
        along[:, at_g, :] = dot(taps_x, pieces(block)).reshape(6, 8, 256)
        return carry

    lax.fori_loop(0, GROUPS, restrict_x, 0, unroll=3)
    part = dot(pieces(along[...].reshape(6 * PAD, 256)), taps_y[...])
    part = (part[: 6 * PAD] + part[6 * PAD : 12 * PAD] + part[12 * PAD :]) * (1.0 / 60.0)
    rest_low[...] = part[:, :128].reshape(6, PAD, 128)
    rest_high[...] = part[:, 128:].reshape(6, PAD, 128)

    pack(0, [[rest_high[r, rows(g), :] for r in range(6)] for g in range(GROUPS)], 2, 14, 1)

    pl.semaphore_wait(barrier, len(partners))

    def remote(source, target, send, recv, device):
        copy = pltpu.make_async_remote_copy(
            src_ref=source,
            dst_ref=target,
            send_sem=send,
            recv_sem=recv,
            device_id=device,
            device_id_type=MESH,
        )
        copy.start()
        return copy

    sent = []

    def inside(dx, dy):
        ok = None
        for here, step, size in ((gx, dx, nx), (gy, dy, ny)):
            if step:
                holds = here > 0 if step < 0 else here < size - 1
                ok = holds if ok is None else ok & holds
        return ok

    def send(moves):
        copies = []
        for dx, dy, source, target, send_sem, recv_sem in moves:
            copy = pltpu.make_async_remote_copy(
                src_ref=source,
                dst_ref=target,
                send_sem=send_sem,
                recv_sem=recv_sem,
                device_id=at(dx, dy),
                device_id_type=MESH,
            )
            pl.when(inside(dx, dy))(copy.start)
            copies.append((dx, dy, copy))
        sent.extend(copies)
        return copies

    def row_moves(e, to_left, at_right, to_right, at_left):
        return [
            (-1, 0, to_left, at_right, x_send.at[e, 0], x_recv.at[e, 1]),
            (1, 0, to_right, at_left, x_send.at[e, 1], x_recv.at[e, 0]),
        ]

    def side_moves(e):
        used = pl.ds(0, 8 if e == 0 else 24)
        return [
            (
                -sx,
                -sy,
                packed.at[e, used],
                packed_in.at[e, n, used],
                p_send.at[e, n],
                p_recv.at[e, n],
            )
            for n, (sx, sy) in sorted(enumerate(SIDES), key=lambda side: -abs(side[1][0]))
        ]

    def rim_rows(v):
        return row_moves(4 + v, ured.at[1, v], ured.at[5, v], ured.at[4, v], ured.at[0, v])

    def arrived(copies):
        for dx, dy, copy in copies:
            pl.when(inside(-dx, -dy))(copy.wait_recv)

    def sides(e, count, above):
        result = []
        for sx, ok in ((-1, left_ok), (0, None), (1, right_ok)):
            n = 2 * (sx + 1)
            there = jnp.where(above, high_f, low_f)
            if ok is not None:
                there = there * jnp.where(ok, 1.0, 0.0)
            result.append(
                [
                    jnp.where(
                        there > 0.5,
                        jnp.where(above, packed_in[e, n + 1, rows(v), :], packed_in[e, n, rows(v), :]),
                        0.0,
                    )
                    for v in range(count)
                ]
            )
        return result

    copies = send(
        side_moves(0)[:4]
        + row_moves(0, rest_low.at[0], rim_in.at[1], rest_low.at[5], rim_in.at[0])
        + side_moves(0)[4:]
    )

    for load in loads[2:]:
        load.wait()
    diagonal = iota((PAD, PLANES), 0) == iota((PAD, PLANES), 1)
    coef = jnp.sum(
        jnp.where(diagonal, jnp.broadcast_to(coef_ref[...], (PAD, PLANES)), 0.0),
        axis=1,
        keepdims=True,
    )
    coef_b[...] = jnp.broadcast_to(coef, (PAD, 128))
    coef_a[...] = jnp.broadcast_to(1.0 - 4.0 * coef, (PAD, 128))
    for i in range(4):
        sd[i, :PLANES] = sd_in[:, i, :]
        sd[i, PLANES:] = jnp.zeros((PAD - PLANES, 128), F32)
    cols = col_ref[...]
    cols_t = jnp.transpose(jnp.concatenate([cols.astype(F32), jnp.zeros((120, 128), F32)], axis=0))
    column = iota((512, 128), 0)
    for a in range(8):
        k = pl.ds(128 * a, 128)
        pick[:, k] = jnp.where(column == cols[a : a + 1], 1.0, 0.0).astype(BF16)
        of_slot = jnp.broadcast_to(cols_t[:, a : a + 1], (128, 512))
        place[k, :] = jnp.where(of_slot == iota((128, 512), 1).astype(F32), 1.0, 0.0).astype(BF16)
    obs_scale = prec_ref[...] * live_ref[...].astype(F32)
    scale = [
        jnp.concatenate([obs_scale[2 * n : 2 * n + 1], obs_scale[2 * n + 1 : 2 * n + 2]], axis=1)
        for n in range(4)
    ]

    arrived(copies)

    rim = sides(0, 1, (lane8 & 1) == 0)
    ends = (lane8 == 0) | (lane8 == 127)
    own = [[] for g in range(GROUPS)]
    for g in range(GROUPS):
        first = 14 * g + 1
        for i in range(4):
            value = rest_low[i + 1, rows(g), :]
            tails = roll(rim[1][0], -(first + 2 * (i + 1)))
            if i == 0:
                value = value + jnp.where(left_f > 0.5, rim_in[0, rows(g), :], 0.0)
                tails = tails + roll(rim[0][0], -(first + 10))
            if i == 3:
                value = value + jnp.where(right_f > 0.5, rim_in[1, rows(g), :], 0.0)
                tails = tails + roll(rim[2][0], -first)
            value = sd[i, rows(g), :] * (value + jnp.where(ends, tails, 0.0))
            field[0, 4 + i, rows(g), :] = value
            own[g].append(value)

    def pack_and_send(e, parts):
        pack(1 + e, parts, 8, 32, 4)
        def part(r):
            return field.at[e, pl.ds(r, 2)]

        near = row_moves(1 + e, part(4), part(8), part(6), part(2))
        far = row_moves(7 + e, part(6), part(10), part(4), part(0))
        side = side_moves(1 + e)
        copies = send(side[:4] + near + side[4:] + far)
        return copies[:-2], copies[-2:]

    def smooth(rows, first, coefs):
        result = []
        for n in range(1, len(rows) - 1):
            i = first + n
            a, b, a_high, b_high = coefs[0 if i < 0 else 1 if i < 4 else 2]
            (low, high), before, after = rows[n], rows[n - 1], rows[n + 1]
            of_low, of_high = beside(low, high, lane8)
            of_low = of_low + before[0] + after[0]
            of_high = of_high + before[1] + after[1]
            result.append((a * low + b * of_low, a_high * high + b_high * of_high))
        return result

    def coefficients(g):
        a, b = coef_a[rows(g), :], coef_b[rows(g), :]
        return [(a * f, b * f, a * f * edge_f, b * f * edge_f) for f in (left_f, F32(1.0), right_f)]

    def line(e, g, r):
        low = field[e, r, rows(g), :]
        if r < 4:
            low = jnp.where(left_f > 0.5, low, 0.0)
        if r >= 8:
            low = jnp.where(right_f > 0.5, low, 0.0)
        return low

    def side(tails, g, r):
        return roll(tails[r // 4][g // 4], -(32 * (g % 4) + 8 * (r % 4) + 4))

    def smooth_near(e):
        tails = sides(1 + e, 3, (lane8 & 4) == 4)
        for g in range(GROUPS):
            at_g, coefs = rows(g), coefficients(g)
            lines = [(line(e, g, r), side(tails, g, r)) for r in range(2, 10)]
            for n, k in enumerate((0, 1, 6, 7)):
                high_in[n, at_g, :] = lines[k][1]
            once = smooth(lines, -2, coefs)
            for n, k in enumerate((0, 1, 4, 5)):
                once_low[n, at_g, :], once_high[n, at_g, :] = once[k]
            for i, (low, high) in enumerate(smooth(once, -1, coefs)):
                base[e, i, at_g, :] = low
                base_high[i, at_g, :] = high

    def smooth_far(e):
        tails = sides(1 + e, 3, (lane8 & 4) == 4)
        for g in range(GROUPS):
            at_g, coefs = rows(g), coefficients(g)
            above = [(line(e, g, r), side(tails, g, r)) for r in (0, 1)]
            above += [(line(e, g, 2 + n), high_in[n, at_g, :]) for n in (0, 1)]
            below = [(line(e, g, 6 + n), high_in[n, at_g, :]) for n in (2, 3)]
            below += [(line(e, g, r), side(tails, g, r)) for r in (10, 11)]
            once = [(once_low[n, at_g, :], once_high[n, at_g, :]) for n in range(4)]
            above = smooth(smooth(above, -4, coefs) + once[:2], -3, coefs)
            below = smooth(once[2:] + smooth(below, 4, coefs), 3, coefs)
            own = [(base[e, i, at_g, :], base_high[i, at_g, :]) for i in range(4)]
            values = smooth(smooth(above + own + below, -2, coefs), -1, coefs)
            for i, (low, _) in enumerate(values):
                pushed = sd[i, at_g, :] * low
                ured[1 + i, e, at_g, :] = pushed
                gathered[at_g, pl.ds(128 * i, 128)] = pushed

    def observe():
        left = pieces(gathered[...])
        seen = []
        for n in range(4):
            k = pl.ds(256 * n, 256)
            taken = dot(left, pick[:, k])
            taken = taken[:MPAD] + taken[MPAD : 2 * MPAD] + taken[2 * MPAD :]
            seen.append(jnp.sum(weight[:, k] * taken[:PLANES], axis=0, keepdims=True))
        return seen

    def scatter(seen):
        for n in range(4):
            k = pl.ds(256 * n, 256)
            back = weight[:, k] * (seen[n] * scale[n] * SCALE)
            back = jnp.concatenate([back, jnp.zeros((MPAD - PLANES, 256), F32)], axis=0)
            scaled[:, k] = pieces(back)

    def products(seen):
        parts = []
        for i, j in PAIRS:
            total = jnp.zeros((8, 128), F32)
            for g in range(GROUPS):
                for row in range(4):
                    total = total + base[i, row, rows(g), :] * base[j, row, rows(g), :]
            parts.append(jnp.sum(total, axis=0, keepdims=True))
        whole = []
        for (i, j), part in zip(PAIRS, parts):
            for n in range(4):
                square = scale[n] * seen[i][n] * seen[j][n]
                part = part + square[:, :128] + square[:, 128:]
            whole.append(part)
        whole += parts[:3]
        whole.append(jnp.zeros((16 - len(whole), 128), F32))
        total = jnp.sum(jnp.concatenate(whole, axis=0), axis=1, keepdims=True)
        mine = iota((16, 128), 0) == (iota((16, 128), 1) >> 3)
        msg_a[...] = jnp.sum(jnp.where(mine, total, 0.0), axis=0, keepdims=True)

    def put_back(e):
        own = [[] for g in range(GROUPS)]
        for h in range(2):
            value = dot(scaled[...], place[:, 256 * h : 256 * h + 256])
            value = value[:PAD] + value[MPAD : MPAD + PAD] + value[2 * MPAD : 2 * MPAD + PAD]
            for i in (2 * h, 2 * h + 1):
                row = sd[i] * value[:, 128 * (i % 2) : 128 * (i % 2) + 128]
                field[e, 4 + i] = row
                for g in range(GROUPS):
                    own[g].append(row[8 * g : 8 * g + 8])
        return own

    def reduce_start(msg, slots, send_sem, recv_sem, size, mine, partner):
        slots[mine] = msg[...]
        for o in sorted(range(1, size), key=lambda o: -min(o, size - o)):
            pltpu.make_async_remote_copy(
                src_ref=msg,
                dst_ref=slots.at[mine],
                send_sem=send_sem,
                recv_sem=recv_sem,
                device_id=partner(o),
                device_id_type=MESH,
            ).start()

    def all_of(slots, send_sem, recv_sem, size, partner):
        several = slots.at[pl.ds(0, size - 1)]
        return pltpu.make_async_remote_copy(
            src_ref=several,
            dst_ref=several,
            send_sem=send_sem,
            recv_sem=recv_sem,
            device_id=partner(1),
            device_id_type=MESH,
        )

    def total_of(slots, size):
        totals = [slots[o] for o in range(size)]
        while len(totals) > 1:
            totals = [sum(totals[n : n + 2]) for n in range(0, len(totals), 2)]
        return totals[0]

    def over_y(o):
        return at(0, o)

    def over_x(o):
        return at(o, 0)

    near, far = pack_and_send(0, own)
    arrived(near)
    smooth_near(0)
    arrived(far)
    smooth_far(0)
    seen = [observe()]
    scatter(seen[0])
    near, far = pack_and_send(1, put_back(1))
    arrived(near)
    smooth_near(1)
    arrived(far)
    rims = send(rim_rows(0))
    smooth_far(1)
    seen.append(observe())
    scatter(seen[1])
    near, far = pack_and_send(2, put_back(2))
    arrived(near)
    smooth_near(2)
    arrived(far)
    rims += send(rim_rows(1))
    smooth_far(2)
    edges = [
        [ured[1 + i, v, rows(g), :] for v in range(3) for i in range(4)] for g in range(GROUPS)
    ]
    pack(4, edges, 2, 32, 1)
    rims += send(side_moves(4) + rim_rows(2))
    seen.append(observe())
    products(seen)
    reduce_start(msg_a, slots_a, a_send, a_recv, ny, gy, over_y)

    for v in range(3):
        for i in range(4):
            ctl[v, i] = base[v, i]
    sums_a = all_of(slots_a, a_send, a_recv, ny, over_y)
    sums_a.wait_recv()
    msg_b[...] = total_of(slots_a, ny)
    reduce_start(msg_b, slots_b, b_send, b_recv, nx, gx, over_x)
    arrived(rims)
    tails = sides(4, 3, (lane8 & 1) == 1)
    out_row, in_col = iota((128, 48), 0), iota((128, 48), 1)
    off = (out_row & 15) - 4 * ((in_col >> 3) - 1)
    spread_x = jnp.where((in_col & 7) == (out_row >> 4), tap(off, 4), 0.0).astype(BF16)
    spread_x = jnp.concatenate([spread_x] * 3, axis=1)
    spread_y = tap(iota((256, 256), 1) - 2 * coarse_lane(iota((256, 256), 0)), 2).astype(BF16)
    sides_in = (lane8 == 0) | (lane8 == 127)

    def interpolate(v):
        for g in range(GROUPS):
            for r in range(6):
                value = ured[r, v, rows(g), :]
                if r == 0:
                    value = jnp.where(left_f > 0.5, value, 0.0)
                if r == 5:
                    value = jnp.where(right_f > 0.5, value, 0.0)
                sx = 0 if r == 0 else 2 if r == 5 else 1
                shift = 32 * (g % 4) + 8 * v + 2 * ((r - 1) % 4) + 1
                end = jnp.where(sides_in, roll(tails[sx][g // 4], -shift), 0.0)
                along[r, rows(g), :] = jnp.concatenate([value, end], axis=1)
        out = dot(pieces(along[...].reshape(6 * PAD, 256)), spread_y)
        out = (out[: 6 * PAD] + out[6 * PAD : 12 * PAD] + out[12 * PAD :]) * (1.0 / 60.0)
        out = out.reshape(6, PAD, 256)
        for g in range(GROUPS):
            part = dot(spread_x, pieces(out[:, 8 * g : 8 * g + 8, :].reshape(48, 256)))
            fine[v, rows(g)] = part.reshape(8, 16, 256)

    interpolate(0)
    interpolate(1)
    interpolate(2)
    sums_b = all_of(slots_b, b_send, b_recv, nx, over_x)
    sums_b.wait_recv()
    total = jnp.broadcast_to(total_of(slots_b, nx), (16, 128))
    mine = iota((16, 128), 0) * 8 == iota((16, 128), 1)
    total = jnp.sum(jnp.where(mine, total, 0.0), axis=1, keepdims=True)
    m00, m01, m02, m11, m12, m22, b0, b1, b2 = [
        jnp.broadcast_to(total[n : n + 1], (8, 128)) for n in range(9)
    ]

    def ratio(a, b):
        return jnp.where(b > 0.0, a / jnp.where(b > 0.0, b, 1.0), 0.0)

    l01, l02 = ratio(m01, m00), ratio(m02, m00)
    m11, m12, m22 = m11 - l01 * m01, m12 - l01 * m02, m22 - l02 * m02
    l12 = ratio(m12, m11)
    b1, b2 = b1 - l01 * b0, b2 - l02 * b0
    c2 = ratio(b2 - l12 * b1, m22 - l12 * m12)
    c1 = ratio(b1, m11) - l12 * c2
    steps[0] = ratio(b0, m00) - l01 * c1 - l02 * c2
    steps[1] = c1
    steps[2] = c2

    for dx, dy, copy in sent:
        pl.when(inside(dx, dy))(copy.wait_send)
    sums_a.wait_send()
    sums_b.wait_send()


def finish(parts, ctl, steps, fine_hbm, control, fine, sems):
    each = [jnp.concatenate([steps[v], steps[v]], axis=1) for v in range(3)]
    copies = []
    for g in range(GROUPS):
        count = min(8, PLANES - 8 * g)
        for p in range(8 * g, 8 * g + count):
            for h in range(2):
                at_h = pl.ds(8 * h, 8)
                fine[p, at_h, :] = sum(each[v] * parts[v, p, at_h, :] for v in range(3))
        planes = pl.ds(8 * g, count)
        copies.append(pltpu.make_async_copy(fine.at[planes], fine_hbm.at[planes], sems.at[g]))
        copies[-1].start()
    for i in range(4):
        value = sum(steps[v][:1] * ctl[v, i] for v in range(3))
        control[:, i, :] = value[:PLANES]
    for copy in copies:
        copy.wait()


def per_device(
    nx, ny, innovation, area, spread_sd, smooth_coef, obs_column, obs_weight, obs_precision, obs_live
):
    vmem, anywhere = pl.BlockSpec(memory_space=pltpu.VMEM), pl.BlockSpec(memory_space=pl.ANY)
    dma = pltpu.SemaphoreType.DMA
    fine, ctl, steps = pl.pallas_call(
        functools.partial(solve, nx, ny),
        out_shape=[
            jax.ShapeDtypeStruct((3, PAD, 16, 256), F32),
            jax.ShapeDtypeStruct((3, 4, PAD, 128), F32),
            jax.ShapeDtypeStruct((3, 8, 128), F32),
        ],
        in_specs=[pl.BlockSpec(memory_space=pltpu.HBM)] * 8,
        out_specs=[vmem, vmem, vmem],
        scratch_shapes=[
            pltpu.VMEM((PAD, 16, 256), F32),
            pltpu.VMEM((16, 256), F32),
            pltpu.VMEM((PLANES, 4, 128), F32),
            pltpu.VMEM((4, PAD, 128), F32),
            pltpu.VMEM((PLANES, 1024), F32),
            pltpu.VMEM((1, PLANES), F32),
            pltpu.VMEM((8, 128), jnp.int32),
            pltpu.VMEM((8, 128), F32),
            pltpu.VMEM((8, 128), jnp.int32),
            pltpu.VMEM((PAD, 128), F32),
            pltpu.VMEM((PAD, 128), F32),
            pltpu.VMEM((512, 1024), BF16),
            pltpu.VMEM((1024, 512), BF16),
            pltpu.VMEM((256, 256), BF16),
            pltpu.VMEM((6, PAD, 256), F32),
            pltpu.VMEM((6, PAD, 128), F32),
            pltpu.VMEM((6, PAD, 128), F32),
            pltpu.VMEM((2, PAD, 128), F32),
            pltpu.VMEM((3, 12, PAD, 128), F32),
            pltpu.VMEM((5, 24, 128), F32),
            pltpu.VMEM((5, 6, 24, 128), F32),
            pltpu.VMEM((3, 4, PAD, 128), F32),
            pltpu.VMEM((4, PAD, 128), F32),
            pltpu.VMEM((4, PAD, 128), F32),
            pltpu.VMEM((4, PAD, 128), F32),
            pltpu.VMEM((4, PAD, 128), F32),
            pltpu.VMEM((6, 3, PAD, 128), F32),
            pltpu.VMEM((MPAD, 512), F32),
            pltpu.VMEM((3 * MPAD, 1024), BF16),
            pltpu.VMEM((1, 128), F32),
            pltpu.VMEM((1, 128), F32),
            pltpu.VMEM((ny, 1, 128), F32),
            pltpu.VMEM((nx, 1, 128), F32),
            dma((8,)),
            dma((10, 2)),
            dma((10, 2)),
            dma((5, 6)),
            dma((5, 6)),
            dma,
            dma,
            dma,
            dma,
        ],
        compiler_params=pltpu.CompilerParams(
            collective_id=0, has_side_effects=True, vmem_limit_bytes=40 << 20
        ),
        name="solve",
    )(
        *(
            pltpu.with_memory_space_constraint(operand, pltpu.HBM)
            for operand in (
                innovation,
                area,
                spread_sd,
                smooth_coef.reshape(1, PLANES),
                obs_column.reshape(8, 128),
                obs_weight,
                obs_precision.reshape(8, 128),
                obs_live.reshape(8, 128),
            )
        )
    )
    return pl.pallas_call(
        finish,
        out_shape=[
            jax.ShapeDtypeStruct((PLANES, 16, 256), F32),
            jax.ShapeDtypeStruct((PLANES, 4, 128), F32),
        ],
        in_specs=[vmem, vmem, vmem],
        out_specs=[anywhere, vmem],
        scratch_shapes=[
            pltpu.VMEM((PAD, 16, 256), F32),
            dma((GROUPS,)),
        ],
        compiler_params=pltpu.CompilerParams(vmem_limit_bytes=24 << 20),
        name="finish",
    )(fine, ctl, steps)


def solution(mesh):
    nx, ny = mesh.shape["gx"], mesh.shape["gy"]
    return jax.shard_map(
        functools.partial(per_device, nx, ny),
        mesh=mesh,
        in_specs=(
            P(None, "gx", "gy"),
            P("gx", "gy"),
            P(None, "gx", "gy"),
            P(),
            P(("gx", "gy")),
            P(None, ("gx", "gy")),
            P(("gx", "gy")),
            P(("gx", "gy")),
        ),
        out_specs=(P(None, "gx", "gy"), P(None, "gx", "gy")),
        check_vma=False,
    )
```
